128 devices in a mesh: seq: 32 (over z, y, core), tp: 4 (over x).
Axes of the slice: x: 4, y: 4, z: 4, core: 2. Of those that a mesh axis runs over, the one named last changes fastest.
Arguments:
- queries: bfloat16 [1024, 4096], P('seq', 'tp'), may hold values from -40 to 40
- cache_keys: bfloat16 [131072, 512], P('seq', 'tp'), may hold values from -4 to 4
- cache_values: bfloat16 [131072, 512], P('seq', 'tp'), may hold values from -16 to 16
- new_keys: bfloat16 [1024, 512], P('seq', 'tp'), may hold values from -4 to 4
- new_values: bfloat16 [1024, 512], P('seq', 'tp'), may hold values from -16 to 16
- reach: int32 [1024], replicated, may hold values from 65537 to 131072, as said below
- norm_gain: float32 [4096], replicated, may hold values from 0.1 to 1.9
- gate_weights: float32 [1024, 2], P('seq'), may hold values from 0.1 to 1
- expert_ids: int32 [1024, 2], P('seq'), may hold values from 0 to 7, all different within a row; in each aligned block of 32 rows (0 to 31, 32 to 63, ...) at most 16 rows name the same one
- w_up: bfloat16 [32, 4096, 3072], P('seq', None, 'tp'), may hold values from -0.09375 to 0.09375
- w_down: bfloat16 [32, 3072, 4096], P('seq', 'tp'), may hold values from -0.0546875 to 0.0546875
Outputs:
- attended: bfloat16 [1024, 4096], P('seq', 'tp')
- expert_mix: bfloat16 [1024, 4096], P('seq', 'tp')
The draws below stay inside these ranges and needn't reach their ends.
Inputs may be any that keep to these rules, and one draw needn't show every extreme that they name: `expert_ids`: each row names two different experts. In each aligned block of 32 rows (the rows of one index of seq) no expert is named by more than 16 rows, and in every draw some expert is named by exactly 16 rows of some block. `reach`: the first query token's entry is 131072; the last token's entry is the least allowed.
All inputs are finite; a program needn't handle non-finite values.
Results may differ from the reference program's by a relative error of at most 0.017.
Values may be sent and summed in bfloat16 or wider, within the bound.
No kernel may reach another device: no remote copies, remote signals or barrier semaphores. Data moves between devices by JAX's collectives and lax.ppermute only.
A program may use at most 128 MiB of HBM per device.

```python
import math
import jax
import jax.numpy as jnp
import numpy as np
from jax import lax

HD = 128
HQ = 32
KVH = 4
D = 4096
E = 8
FF = 12288
TOK_DEV = 32
CTX_DEV = 4096
CAP = 16
GROUP = 4
TOKENS = 1024
CTX_ALL = 131072
N_SEQ = 32


def head_scale(exponent):
    heads = (jnp.arange(KVH * HD, dtype=jnp.int32) // HD).astype(jnp.float32)
    return (1.0 + 2.0 * heads / (KVH - 1)) ** exponent


def draw_queries(key, part):
    key = jax.random.fold_in(key, 3)
    table = jnp.clip(3.0 * jax.random.normal(key, (TOKENS, D), jnp.float32), -12.0, 12.0)
    return table.astype(jnp.bfloat16)


def draw_cache_keys(key, part):
    key = jax.random.fold_in(key, 4)
    table = jnp.clip(jax.random.normal(key, (CTX_ALL, KVH * HD), jnp.float32), -4.0, 4.0)
    return table.astype(jnp.bfloat16)


def draw_cache_values(key, part):
    key = jax.random.fold_in(key, 5)
    table = jnp.clip(jax.random.normal(key, (CTX_ALL, KVH * HD), jnp.float32), -4.0, 4.0) * head_scale(1.0)[None, :]
    return table.astype(jnp.bfloat16)


def draw_new_values(key, part):
    key = jax.random.fold_in(key, 6)
    table = jnp.clip(jax.random.normal(key, (TOKENS, KVH * HD), jnp.float32), -4.0, 4.0) * head_scale(1.0)[None, :]
    return table.astype(jnp.bfloat16)


def draw_reach(key, part):
    key = jax.random.fold_in(key, 7)
    least = CTX_ALL - CTX_ALL // 2 + 1
    drawn = CTX_ALL - jax.random.randint(key, (TOKENS,), 0, CTX_ALL // 2)
    drawn = drawn.at[0].set(CTX_ALL)
    drawn = drawn.at[TOKENS - 1].set(least)
    return drawn.astype(jnp.int32)


def shard_levels(key, extent, shards, smallest, largest):
    gain = 1.0
    for dim, blocks in shards:
        steps = jax.random.uniform(jax.random.fold_in(jax.random.fold_in(key, 6), dim), (blocks,), jnp.float32, smallest / len(shards), largest / len(shards))
        gain = gain * jnp.repeat(jnp.exp(steps), extent[dim] // blocks).reshape((-1,) + (1,) * (len(extent) - 1 - dim))
    return gain


def deal_out(stream_key, own, number, rows, amount, top, most, lean):
    sequence = jax.random.permutation(stream_key, amount)
    heavy_load, common = shares(amount, rows * top, most, lean, True), shares(amount, rows * top, most, lean, False)
    places = jnp.arange(amount)

    def named(tallies, offset_by):
        used = int((tallies > 0).sum())
        fixed = max(1, used // 4)
        passed = fixed + (places - fixed + offset_by * (used - fixed)) % max(1, amount - fixed)
        return jnp.zeros((amount,), jnp.int32).at[sequence[jnp.where(places < fixed, places, passed)]].set(jnp.asarray(tallies, jnp.int32))

    tallies = jnp.where(number % 4 == 0, named(heavy_load, number // 4), named(common, number - number // 4 - 1))
    mixed = jax.random.permutation(jax.random.fold_in(own, 3), amount)
    source_of, sink = mixed[0:amount // 2 * 2:2], mixed[1:amount // 2 * 2:2]
    margin = jnp.minimum(tallies[source_of] - 1, most - tallies[sink]) // 2
    margin = jnp.where((source_of == sequence[0]) | (sink == sequence[0]) | (tallies[sink] == 0), 0, jnp.maximum(margin, 0))
    passed = jax.random.randint(jax.random.fold_in(own, 4), (amount // 2,), 0, 1 << 20) % (margin + 1)
    tallies = tallies.at[source_of].add(-passed).at[sink].add(passed)
    items = jnp.searchsorted(jnp.cumsum(tallies), jnp.arange(rows * top), side="right").astype(jnp.int32)
    listing = items.reshape(top, rows).T
    listing = listing[jax.random.permutation(jax.random.fold_in(own, 1), rows)]
    offset_by = jax.random.randint(jax.random.fold_in(own, 2), (rows, 1), 0, top)
    return jnp.take_along_axis(listing, (jnp.arange(top)[None, :] + offset_by) % top, axis=1)


def shares(count, total, most, slope, full):
    loads = [(1 << 20) // math.isqrt(rank ** slope) + 1 for rank in range(1, count + 1)]
    largest = most if full else min(most, max(-(-total // count), total * loads[0] // sum(loads)))
    least = 1 if total - largest >= count - 1 else 0
    holding, surplus = [largest] + [least] * (count - 1), total - largest - least * (count - 1)
    while surplus > 0:
        free = [i for i in range(1, count) if holding[i] < largest] or [i for i in range(1, count) if holding[i] < most]
        pool, budget = sum([loads[i] for i in free]), surplus
        for i in free:
            more = min(most - holding[i], max(1, budget * loads[i] // pool), surplus)
            holding[i] = holding[i] + more
            surplus = surplus - more
    return np.array(holding)


def scatter_about(stream_key, dims, width, bound, shards=(), kind=jnp.bfloat16):
    values = width * jax.random.normal(stream_key, dims, jnp.float32)
    if shards:
        values = values * shard_levels(stream_key, dims, shards, -0.22, 0.18)
    return jnp.clip(values, -bound, bound).astype(kind)


def setup_inputs(seed: int = 0) -> dict:
    keys = jax.random.split(jax.random.key(seed), 12)
    queries = draw_queries(jax.random.fold_in(keys[11], 71), 0)
    cache_keys = draw_cache_keys(jax.random.fold_in(keys[11], 71), 0)
    cache_values = draw_cache_values(jax.random.fold_in(keys[11], 71), 0)
    new_keys = scatter_about(keys[3], (TOKENS, KVH * HD), 1.0, 4.0, ((0, 32), (1, 4)))
    new_values = draw_new_values(jax.random.fold_in(keys[11], 71), 0)
    reach = draw_reach(jax.random.fold_in(keys[11], 71), 0)
    norm_gain = jnp.clip(1.0 + 0.18 * jax.random.normal(keys[6], (D,), jnp.float32), 0.1, 1.9)
    gate_weights = jnp.clip(0.1 + 0.9 * jax.random.uniform(keys[7], (TOKENS, 2), jnp.float32) ** shard_levels(keys[7], (TOKENS, 2), ((0, 32),), -0.2, 0.2), 0.1, 1.0)
    expert_ids_keys = jax.random.split(jax.random.fold_in(keys[8], 1), TOKENS // TOK_DEV)
    expert_ids_turns = jax.random.permutation(jax.random.fold_in(keys[8], 3), TOKENS // TOK_DEV)
    expert_ids = jax.vmap(lambda own, number: deal_out(jax.random.fold_in(keys[8], 2), own, number, TOK_DEV, E, 2, CAP, 2))(expert_ids_keys, expert_ids_turns).reshape((TOKENS, 2))
    w_up = scatter_about(keys[9], (E * GROUP, D, FF // GROUP), D ** -0.5, 0.09375, ((0, 32), (2, 4)))
    w_down = scatter_about(keys[10], (E * GROUP, FF // GROUP, D), FF ** -0.5, 0.0546875, ((0, 32), (1, 4)))
    return dict(queries=queries, cache_keys=cache_keys, cache_values=cache_values, new_keys=new_keys, new_values=new_values, reach=reach, norm_gain=norm_gain, gate_weights=gate_weights, expert_ids=expert_ids, w_up=w_up, w_down=w_down)


EPSILON = 1e-05
MASKED = -1e+30

def block_partial(head_queries, head_keys, head_values, allowed):
    query_count = head_queries.shape[0]
    head_ratio = head_queries.shape[1]
    key_count = head_keys.shape[0]
    flat_queries = head_queries.reshape(query_count * head_ratio, HD)
    scores = lax.dot_general(flat_queries, head_keys, (((1,), (1,)), ((), ())), preferred_element_type=jnp.float32)
    scores = scores.reshape(query_count, head_ratio, key_count) * HD ** (-0.5)
    masked = jnp.where(allowed, scores, MASKED)
    top_score = lax.optimization_barrier(jnp.max(masked, axis=-1))
    weights = jnp.where(allowed, jnp.exp(masked - top_score[..., None]), 0.0)
    weight_sum = lax.optimization_barrier(jnp.sum(weights, axis=-1))
    head_out = jnp.dot(weights.astype(jnp.bfloat16).reshape(query_count * head_ratio, key_count), head_values, preferred_element_type=jnp.float32)
    head_out = head_out.reshape(query_count, head_ratio, HD) / jnp.maximum(weight_sum, 1.0)[..., None]
    return (head_out, top_score, weight_sum)

def attention(queries, cache_keys, cache_values, new_keys, new_values, reach):
    head_ratio = HQ // KVH
    token_ids = jnp.arange(TOKENS, dtype=jnp.int32)

    def one_shard(carry, shard_index):
        running_top, running_sum, running_out = carry
        cache_start = shard_index * CTX_DEV
        window_start = shard_index * TOK_DEV
        shard_keys = jnp.concatenate([lax.dynamic_slice_in_dim(cache_keys, cache_start, CTX_DEV, 0), lax.dynamic_slice_in_dim(new_keys, window_start, TOK_DEV, 0)], axis=0)
        shard_values = jnp.concatenate([lax.dynamic_slice_in_dim(cache_values, cache_start, CTX_DEV, 0), lax.dynamic_slice_in_dim(new_values, window_start, TOK_DEV, 0)], axis=0)
        cache_pos = cache_start + jnp.arange(CTX_DEV, dtype=jnp.int32)
        window_pos = window_start + jnp.arange(TOK_DEV, dtype=jnp.int32)
        visible = jnp.concatenate([cache_pos[None, :] < reach[:, None], window_pos[None, :] <= token_ids[:, None]], axis=1)
        allowed = visible[:, None, :]
        out_list = []
        top_list = []
        sum_list = []
        for kv_head in range(KVH):
            head_queries = queries[:, kv_head * head_ratio * HD:(kv_head + 1) * head_ratio * HD].reshape(TOKENS, head_ratio, HD)
            head_keys = shard_keys[:, kv_head * HD:(kv_head + 1) * HD]
            head_values = shard_values[:, kv_head * HD:(kv_head + 1) * HD]
            head_out, top_score, weight_sum = block_partial(head_queries, head_keys, head_values, allowed)
            out_list.append(head_out)
            top_list.append(top_score)
            sum_list.append(weight_sum)
        shard_out = jnp.concatenate(out_list, axis=1)
        shard_top = jnp.concatenate(top_list, axis=1)
        shard_sum = jnp.concatenate(sum_list, axis=1)
        new_top = jnp.maximum(running_top, shard_top)
        old_scale = jnp.exp(running_top - new_top)
        shard_share = shard_sum * jnp.exp(shard_top - new_top)
        next_sum = running_sum * old_scale + shard_share
        next_out = running_out * old_scale[..., None] + shard_share[..., None] * shard_out
        return ((new_top, next_sum, next_out), None)
    start_carry = (jnp.full((TOKENS, HQ), MASKED, jnp.float32), jnp.zeros((TOKENS, HQ), jnp.float32), jnp.zeros((TOKENS, HQ, HD), jnp.float32))
    final_carry, unused = lax.scan(one_shard, start_carry, jnp.arange(N_SEQ, dtype=jnp.int32))
    total_sum = final_carry[1]
    total_out = final_carry[2]
    return (total_out / total_sum[..., None]).reshape(TOKENS, D).astype(jnp.bfloat16)

def experts(attended, norm_gain, gate_weights, expert_ids, w_up, w_down):
    as_float = attended.astype(jnp.float32)
    inverse = lax.rsqrt(lax.optimization_barrier(jnp.mean(as_float * as_float, axis=1)) + EPSILON)
    normed = (as_float * inverse[:, None] * norm_gain[None, :]).astype(jnp.bfloat16)
    limit = N_SEQ * CAP

    def one_expert(running, expert):
        up_block = lax.dynamic_slice_in_dim(w_up, expert * GROUP, GROUP, 0)
        up_full = jnp.transpose(up_block, (1, 0, 2)).reshape(D, FF)
        down_full = lax.dynamic_slice_in_dim(w_down, expert * GROUP, GROUP, 0).reshape(FF, D)
        chosen = expert_ids == expert
        member = jnp.any(chosen, axis=1)
        row_order = jnp.argsort(jnp.where(member, 0, 1).astype(jnp.int32), stable=True)[:limit]
        gate_share = lax.optimization_barrier(jnp.sum(jnp.where(chosen, gate_weights, 0.0), axis=1))
        picked_rows = normed[row_order]
        hidden = jax.nn.silu(jnp.dot(picked_rows, up_full, preferred_element_type=jnp.float32)).astype(jnp.bfloat16)
        result = jnp.dot(hidden, down_full, preferred_element_type=jnp.float32)
        return (running.at[row_order].add(result * gate_share[row_order][:, None]), None)
    total, unused = lax.scan(one_expert, jnp.zeros((TOKENS, D), jnp.float32), jnp.arange(E, dtype=jnp.int32))
    return total.astype(jnp.bfloat16)

def reference(queries, cache_keys, cache_values, new_keys, new_values, reach, norm_gain, gate_weights, expert_ids, w_up, w_down):
    attended = attention(queries, cache_keys, cache_values, new_keys, new_values, reach)
    expert_mix = experts(attended, norm_gain, gate_weights, expert_ids, w_up, w_down)
    return (attended, expert_mix)
```

```python
import functools
import math

import jax
import jax.numpy as jnp
from jax import lax
from jax.experimental import pallas as pl
from jax.experimental.pallas import tpu as pltpu
from jax.sharding import PartitionSpec as P

HD = 128
E = 8
CAP = 16
EPSILON = 1e-05
NEG = -1e30
FLOOR = -1e20
BF = jnp.bfloat16
F32 = jnp.float32
SCALE = HD**-0.5 * math.log2(math.e)
MIB = 1024 * 1024
VM = pl.BlockSpec(memory_space=pltpu.VMEM)
SM = pl.BlockSpec(memory_space=pltpu.SMEM)

def attn_kernel(pos_ref, lim_ref, q_ref, k0_ref, k1_ref, v0_ref, v1_ref, nk_ref, nv_ref, o_ref, kk, vv, s_scr, m_scr, l_scr, *, R, CH, W):
    T=q_ref.shape[0]; KEYS=k0_ref.shape[0]; NT=(T//R)*8; NCH=KEYS//CH; WIN=2*KEYS
    for half,kr,vr in ((0,k0_ref,v0_ref),(1,k1_ref,v1_ref)):
        k=kr[...]; v=vr[...]
        kk[pl.ds(half*KEYS,KEYS),:]=jnp.concatenate([k,k],axis=1)
        vv[pl.ds(half*KEYS,KEYS),:]=jnp.concatenate([v,jnp.ones_like(v)],axis=1)
    nk=nk_ref[...]; nv=nv_ref[...]
    zero=jnp.zeros((128-2*W,HD),BF)
    nk=jnp.concatenate([nk,zero],axis=0); nv=jnp.concatenate([nv,zero],axis=0)
    kk[pl.ds(WIN,128),:]=jnp.concatenate([nk,nk],axis=1)
    vv[pl.ds(WIN,128),:]=jnp.concatenate([nv,jnp.ones_like(nv)],axis=1)
    l_scr[...]=jnp.zeros_like(l_scr)
    def tile(i):
        h=lax.rem(i,8); tb=lax.div(i,8)
        return pl.multiple_of(tb*R,R), pl.multiple_of(h*HD,HD), h
    def load_q(i):
        r,c,_=tile(i)
        qf=q_ref[pl.ds(r,R),pl.ds(c,HD)].astype(F32)*SCALE
        hi=qf.astype(BF); lo=(qf-hi.astype(F32)).astype(BF)
        return jnp.concatenate([hi,lo],axis=1)
    def dotk(qq,k):
        return lax.dot_general(qq,k,(((1,),(1,)),((),())),preferred_element_type=F32)
    def window_scores(i, qq):
        r,_,_=tile(i)
        s=dotk(qq,kk[pl.ds(WIN,128),:])
        lane=lax.broadcasted_iota(jnp.int32,(R,128),1)
        row=lax.broadcasted_iota(jnp.int32,(R,128),0)+r
        tok=lax.div(row,W)*(2*W)+lax.rem(row,W)+pos_ref[4]*W
        key=jnp.where(lane<W,lane+pos_ref[2],lane-W+pos_ref[3])
        return jnp.where((lane<2*W)&(key<=tok),s,NEG)
    def step(i, slot, do_qk, do_pv):
        if do_qk:
            qq=load_q(i+1)
            r1,_,_=tile(i+1)
            lim=lim_ref[pl.ds(r1,R),:]
            lane0=lax.broadcasted_iota(jnp.int32,(R,128),1)
            mx=jnp.full((R,128),FLOOR,F32)
            sw=window_scores(i+1,qq)
            s_scr[1-slot,:,pl.ds(WIN,128)]=sw
            mx=jnp.maximum(mx,sw)
        if do_pv:
            m=m_scr[...]
            p=jnp.exp2(s_scr[slot,:,pl.ds(WIN,128)]-m)
            acc=jnp.dot(p.astype(BF),vv[pl.ds(WIN,128),:],preferred_element_type=F32)
        for half in range(2):
            if do_qk:
                limh=lim-pos_ref[half]
            for j in range(NCH):
                ks=half*KEYS+j*CH
                if do_qk:
                    s=dotk(qq,kk[pl.ds(ks,CH),:])
                    for c in range(CH//128):
                        sc=jnp.where(lane0+(j*CH+c*128)<limh,s[:,c*128:(c+1)*128],NEG)
                        s_scr[1-slot,:,pl.ds(ks+c*128,128)]=sc
                        mx=jnp.maximum(mx,sc)
                if do_pv:
                    p=jnp.concatenate([jnp.exp2(s_scr[slot,:,pl.ds(ks+c*128,128)]-m).astype(BF) for c in range(CH//128)],axis=1)
                    acc=acc+jnp.dot(p,vv[pl.ds(ks,CH),:],preferred_element_type=F32)
        if do_pv:
            r,c,h=tile(i)
            l=acc[:,HD:]
            o_ref[pl.ds(r,R),pl.ds(c,HD)]=(acc[:,:HD]/jnp.maximum(l,1.0)).astype(BF)
            L=jnp.where(l>0,m+jnp.log2(jnp.maximum(l,1e-30)),NEG)
            lane=lax.broadcasted_iota(jnp.int32,(R,128),1)
            l_scr[pl.ds(r,R),:]=jnp.where(lax.rem(lane,8)==h,L,l_scr[pl.ds(r,R),:])
        if do_qk:
            m_scr[...]=jnp.broadcast_to(jnp.max(mx,axis=1,keepdims=True),(R,128))
    step(jnp.int32(-1),1,True,False)
    def two(t,_):
        step(2*t,0,True,True)
        step(2*t+1,1,True,True)
        return 0
    lax.fori_loop(0,NT//2-1,two,0)
    step(jnp.int32(NT-2),0,True,True)
    step(jnp.int32(NT-1),1,False,True)
    L=l_scr[...]
    hi=L.astype(BF); mid=(L-hi.astype(F32)).astype(BF); lo=(L-hi.astype(F32)-mid.astype(F32)).astype(BF)
    lane=lax.broadcasted_iota(jnp.int32,L.shape,1)
    o_ref[:,pl.ds(8*HD,128)]=jnp.where(lane<8,hi.astype(F32),jnp.where(lane<16,mid.astype(F32),jnp.where(lane<24,lo.astype(F32),0.0))).astype(BF)

def attention(pos, lim, q, k0, k1, v0, v1, nk, nv, R=256, CH=512):
    T=q.shape[0]; KEYS=k0.shape[0]; W=nk.shape[0]//2
    return pl.pallas_call(
        functools.partial(attn_kernel,R=R,CH=CH,W=W),
        out_shape=jax.ShapeDtypeStruct((T,9*HD),BF),
        in_specs=[SM]+[VM]*8,
        out_specs=VM,
        scratch_shapes=[pltpu.VMEM((2*KEYS+128,2*HD),BF),pltpu.VMEM((2*KEYS+128,2*HD),BF),
            pltpu.VMEM((2,R,2*KEYS+128),F32),pltpu.VMEM((R,128),F32),pltpu.VMEM((T,128),F32)],
        compiler_params=pltpu.CompilerParams(vmem_limit_bytes=60*MIB),
        cost_estimate=pl.CostEstimate(flops=4*T*8*2*KEYS*HD*2,bytes_accessed=8*1024*1024,transcendentals=T*8*2*KEYS),
    )(pos,lim,q,k0,k1,v0,v1,nk,nv)


def home_kernel(recv_ref, ids_ref, att_ref, msg_ref):
    blocks, tok, _ = recv_ref.shape
    heads = att_ref.shape[1] // HD
    logs = []
    for s in range(blocks):
        tail = recv_ref[s, :, pl.ds(heads * HD, 128)].astype(F32)
        logs.append(tail + pltpu.roll(tail, 120, 1) + pltpu.roll(tail, 112, 1))
    top = functools.reduce(jnp.maximum, logs)
    shares = [jnp.exp2(x - top) for x in logs]
    inverse = 1.0 / functools.reduce(jnp.add, shares)
    shares = [x * inverse for x in shares]
    for h in range(heads):
        total = jnp.zeros((tok, HD), F32)
        for s in range(blocks):
            total = total + shares[s][:, h : h + 1] * recv_ref[s, :, pl.ds(h * HD, HD)].astype(F32)
        att_ref[:, pl.ds(h * HD, HD)] = total.astype(BF)
    slot = lax.broadcasted_iota(jnp.int32, (E * CAP, tok), 0)
    expert = lax.div(slot, CAP)
    member = (ids_ref[0:1, :] == expert) | (ids_ref[1:2, :] == expert)
    earlier = lax.broadcasted_iota(jnp.int32, (tok, tok), 0) < lax.broadcasted_iota(jnp.int32, (tok, tok), 1)
    rank = jnp.dot(
        jnp.where(member, 1.0, 0.0).astype(BF), jnp.where(earlier, 1.0, 0.0).astype(BF), preferred_element_type=F32
    )
    placing = member & (rank == lax.rem(slot, CAP).astype(F32))
    rows = jnp.dot(
        jnp.where(placing, 1.0, 0.0).astype(BF), att_ref[...], preferred_element_type=F32
    ).astype(BF)
    half = rows.shape[1] // 2
    for e in range(E):
        for c in range(2):
            part = rows[e * CAP : (e + 1) * CAP, c * half : (c + 1) * half]
            for y in range(msg_ref.shape[1]):
                for x in range(msg_ref.shape[3]):
                    msg_ref[e, y, c, x] = part


def home(recv, ids_t, tp):
    tok, width = recv.shape[1], recv.shape[2] - 128
    return pl.pallas_call(
        home_kernel,
        out_shape=(
            jax.ShapeDtypeStruct((tok, width), BF),
            jax.ShapeDtypeStruct((E, 2, 2, tp, CAP, width // 2), BF),
        ),
        in_specs=[VM, VM],
        out_specs=(VM, VM),
        compiler_params=pltpu.CompilerParams(vmem_limit_bytes=32 * MIB),
    )(recv, ids_t)


def up_kernel(core_ref, own_ref, other_ref, gain_ref, up_ref, down_ref, hidden_ref, send_ref):
    seqs, tp, cap, half = own_ref.shape
    rows = seqs * cap
    core = core_ref[0]

    def part(ref, x):
        return ref[:, x].reshape(rows, half).astype(F32)

    square = jnp.zeros((rows, 128), F32)
    for ref in (own_ref, other_ref):
        for x in range(tp):
            a = part(ref, x)
            a = a * a
            for c in range(half // 128):
                square = square + a[:, c * 128 : (c + 1) * 128]
    mean = jnp.sum(square, axis=1, keepdims=True) / (2 * tp * half)
    inverse = lax.rsqrt(mean + EPSILON)
    total = jnp.zeros((rows, up_ref.shape[1]), F32)
    for ref, side in ((own_ref, core), (other_ref, 1 - core)):
        for x in range(tp):
            first = pl.multiple_of(x * 2 * half + side * half, half)
            normed = (part(ref, x) * inverse * gain_ref[:, pl.ds(first, half)]).astype(BF)
            total = total + jnp.dot(normed, up_ref[pl.ds(first, half), :], preferred_element_type=F32)
    hidden = (total / (1.0 + jnp.exp(-total))).astype(BF)
    hidden_ref[...] = hidden
    for x in range(tp):
        first = pl.multiple_of(x * 2 * half + (1 - core) * half, half)
        out = jnp.dot(hidden, down_ref[:, pl.ds(first, half)], preferred_element_type=F32)
        send_ref[:, x] = out.astype(BF).reshape(seqs, cap, half)


def up_project(core, own, other, gain, w_up, w_down):
    rows = own.shape[0] * own.shape[2]
    return pl.pallas_call(
        up_kernel,
        out_shape=(
            jax.ShapeDtypeStruct((rows, w_up.shape[1]), BF),
            jax.ShapeDtypeStruct(own.shape, BF),
        ),
        in_specs=[SM] + [VM] * 5,
        out_specs=(VM, VM),
        compiler_params=pltpu.CompilerParams(vmem_limit_bytes=48 * MIB),
    )(core, own, other, gain, w_up, w_down)


def down_kernel(core_ref, hidden_ref, down_ref, partner_ref, out_ref):
    seqs, tp, cap, half = out_ref.shape
    hidden = hidden_ref[...]
    for x in range(tp):
        first = pl.multiple_of(x * 2 * half + core_ref[0] * half, half)
        out = jnp.dot(hidden, down_ref[:, pl.ds(first, half)], preferred_element_type=F32)
        out = out + partner_ref[:, x].reshape(seqs * cap, half).astype(F32)
        out_ref[:, x] = out.astype(BF).reshape(seqs, cap, half)


def down_project(core, hidden, w_down, partner):
    return pl.pallas_call(
        down_kernel,
        out_shape=jax.ShapeDtypeStruct(partner.shape, BF),
        in_specs=[SM] + [VM] * 3,
        out_specs=VM,
        compiler_params=pltpu.CompilerParams(vmem_limit_bytes=40 * MIB),
    )(core, hidden, w_down, partner)


def mix_kernel(recv_ref, ids_ref, gate_ref, out_ref):
    experts, pair, cores, tp, cap, half = recv_ref.shape
    tok = ids_ref.shape[0]
    terms = experts * pair * tp * cap
    lane = lax.broadcasted_iota(jnp.int32, (tok, terms), 1)
    expert = lax.div(lane, pair * tp * cap)
    first, second = ids_ref[:, 0:1] == expert, ids_ref[:, 1:2] == expert
    gate = jnp.where(first, gate_ref[:, 0:1], 0.0) + jnp.where(second, gate_ref[:, 1:2], 0.0)
    earlier = lax.broadcasted_iota(jnp.int32, (tok, tok), 1) < lax.broadcasted_iota(jnp.int32, (tok, tok), 0)
    rank = jnp.dot(
        jnp.where(earlier, 1.0, 0.0).astype(BF), jnp.where(first | second, 1.0, 0.0).astype(BF), preferred_element_type=F32
    )
    gate = jnp.where(rank == lax.rem(lane, cap).astype(F32), gate, 0.0)
    high = gate.astype(BF)
    low = (gate - high.astype(F32)).astype(BF)
    both = jnp.concatenate([high, low], axis=0)
    for c in range(cores):
        values = recv_ref[:, :, c].reshape(terms, half)
        out = jnp.dot(both, values, preferred_element_type=F32)
        out_ref[:, pl.ds(c * half, half)] = (out[:tok] + out[tok:]).astype(BF)


def mix(recv, ids, gates):
    return pl.pallas_call(
        mix_kernel,
        out_shape=jax.ShapeDtypeStruct((ids.shape[0], 2 * recv.shape[5]), BF),
        in_specs=[VM] * 3,
        out_specs=VM,
        compiler_params=pltpu.CompilerParams(vmem_limit_bytes=32 * MIB),
    )(recv, ids, gates)


def per_device(
    queries, cache_keys, cache_values, new_keys, new_values, reach, norm_gain, gate_weights, expert_ids, w_up, w_down
):
    seqs, tp = lax.axis_size("seq"), lax.axis_size("tp")
    seq = lax.axis_index("seq")
    core = lax.rem(seq, 2)
    partner = seq + 1 - 2 * core
    tok, width = queries.shape
    ctx = cache_keys.shape[0]
    chips = seqs // 2
    same_core = [list(range(c, seqs, 2)) for c in range(2)]
    swap = [(i, i ^ 1) for i in range(seqs)]

    def swapped(value):
        return lax.ppermute(value, "seq", swap)

    other_keys, other_values = swapped(cache_keys), swapped(cache_values)
    other_new_keys, other_new_values = swapped(new_keys), swapped(new_values)
    all_queries = lax.all_to_all(
        jnp.broadcast_to(queries[None], (chips, tok, width)),
        "seq", 0, 0, axis_index_groups=same_core, tiled=True,
    ).reshape(chips * tok, width)
    limits = lax.dynamic_index_in_dim(reach.reshape(chips, 2, tok), core, 1, keepdims=False)
    limits = jnp.broadcast_to(limits.reshape(chips * tok, 1), (chips * tok, 128))
    places = jnp.stack([seq * ctx, partner * ctx, seq * tok, partner * tok, core]).astype(jnp.int32)
    outs = attention(
        places, limits, all_queries, cache_keys, other_keys, cache_values, other_values,
        jnp.concatenate([new_keys, other_new_keys], axis=0),
        jnp.concatenate([new_values, other_new_values], axis=0),
    )
    arrived = lax.all_to_all(
        outs.reshape(chips, tok, outs.shape[1]), "seq", 0, 0, axis_index_groups=same_core, tiled=True
    )
    attended, message = home(arrived, expert_ids.T, tp)
    half = width // 2
    rows = lax.all_to_all(
        message.reshape(seqs * tp, CAP, half), ("seq", "tp"), 0, 0, tiled=True
    ).reshape(seqs, tp, CAP, half)
    side = core.astype(jnp.int32).reshape(1)
    hidden, send = up_project(side, rows, swapped(rows), norm_gain.reshape(1, -1), w_up[0], w_down[0])
    result = down_project(side, hidden, w_down[0], swapped(send))
    returned = lax.all_to_all(
        result.reshape(seqs * tp, CAP, half), ("seq", "tp"), 0, 0, tiled=True
    ).reshape(E, 2, 2, tp, CAP, half)
    return attended, mix(returned, expert_ids, gate_weights)


def solution(mesh):
    placed = (
        P("seq", "tp"),
        P("seq", "tp"),
        P("seq", "tp"),
        P("seq", "tp"),
        P("seq", "tp"),
        P(),
        P(),
        P("seq", None),
        P("seq", None),
        P("seq", None, "tp"),
        P("seq", "tp", None),
    )
    return jax.shard_map(
        per_device,
        mesh=mesh,
        in_specs=placed,
        out_specs=(P("seq", "tp"), P("seq", "tp")),
        check_vma=False,
    )
```

```python
import functools
import math

import jax
import jax.numpy as jnp
from jax import lax
from jax.experimental import pallas as pl
from jax.experimental.pallas import tpu as pltpu
from jax.sharding import PartitionSpec as P

HD = 128
E = 8
CAP = 16
EPSILON = 1e-05
NEG = -1e30
FLOOR = -1e20
BF = jnp.bfloat16
F32 = jnp.float32
SCALE = HD**-0.5 * math.log2(math.e)
MIB = 1024 * 1024
VM = pl.BlockSpec(memory_space=pltpu.VMEM)
SM = pl.BlockSpec(memory_space=pltpu.SMEM)

def attn_kernel(pos_ref, reach_ref, q_ref, k0_ref, k1_ref, v0_ref, v1_ref, nk_ref, nv_ref, o_ref, kk, vv, s_scr, m_scr, l_scr, lim_ref, *, R, CH, W):
    T=q_ref.shape[0]; KEYS=k0_ref.shape[0]; NT=(T//R)*8; NCH=KEYS//CH; WIN=2*KEYS
    for half,kr,vr in ((0,k0_ref,v0_ref),(1,k1_ref,v1_ref)):
        k=kr[...]; v=vr[...]
        kk[pl.ds(half*KEYS,KEYS),:]=jnp.concatenate([k,k],axis=1)
        vv[pl.ds(half*KEYS,KEYS),:]=jnp.concatenate([v,jnp.ones_like(v)],axis=1)
    nk=nk_ref[...]; nv=nv_ref[...]
    zero=jnp.zeros((128-2*W,HD),BF)
    nk=jnp.concatenate([nk,zero],axis=0); nv=jnp.concatenate([nv,zero],axis=0)
    kk[pl.ds(WIN,128),:]=jnp.concatenate([nk,nk],axis=1)
    vv[pl.ds(WIN,128),:]=jnp.concatenate([nv,jnp.ones_like(nv)],axis=1)
    l_scr[...]=jnp.zeros_like(l_scr)
    for t in range(T//R):
        lim_ref[pl.ds(t*R,R),:]=jnp.transpose(jnp.broadcast_to(reach_ref[:,pl.ds(t*R,R)],(128,R)))
    def tile(i):
        h=lax.rem(i,8); tb=lax.div(i,8)
        return pl.multiple_of(tb*R,R), pl.multiple_of(h*HD,HD), h
    def load_q(i):
        r,c,_=tile(i)
        qf=q_ref[pl.ds(r,R),pl.ds(c,HD)].astype(F32)*SCALE
        hi=qf.astype(BF); lo=(qf-hi.astype(F32)).astype(BF)
        return jnp.concatenate([hi,lo],axis=1)
    def dotk(qq,k):
        return lax.dot_general(qq,k,(((1,),(1,)),((),())),preferred_element_type=F32)
    def window_scores(i, qq):
        r,_,_=tile(i)
        s=dotk(qq,kk[pl.ds(WIN,128),:])
        lane=lax.broadcasted_iota(jnp.int32,(R,128),1)
        row=lax.broadcasted_iota(jnp.int32,(R,128),0)+r
        tok=lax.div(row,W)*(2*W)+lax.rem(row,W)+pos_ref[4]*W
        key=jnp.where(lane<W,lane+pos_ref[2],lane-W+pos_ref[3])
        return jnp.where((lane<2*W)&(key<=tok),s,NEG)
    def step(i, slot, do_qk, do_pv):
        if do_qk:
            qq=load_q(i+1)
            r1,_,_=tile(i+1)
            lim=lim_ref[pl.ds(r1,R),:]
            lane0=lax.broadcasted_iota(jnp.int32,(R,128),1)
            mx=jnp.full((R,128),FLOOR,F32)
            sw=window_scores(i+1,qq)
            s_scr[1-slot,:,pl.ds(WIN,128)]=sw
            mx=jnp.maximum(mx,sw)
        if do_pv:
            m=m_scr[...]
            p=jnp.exp2(s_scr[slot,:,pl.ds(WIN,128)]-m)
            acc=jnp.dot(p.astype(BF),vv[pl.ds(WIN,128),:],preferred_element_type=F32)
        for half in range(2):
            if do_qk:
                limh=lim-pos_ref[half]
            for j in range(NCH):
                ks=half*KEYS+j*CH
                if do_qk:
                    s=dotk(qq,kk[pl.ds(ks,CH),:])
                    for c in range(CH//128):
                        sc=jnp.where(lane0+(j*CH+c*128)<limh,s[:,c*128:(c+1)*128],NEG)
                        s_scr[1-slot,:,pl.ds(ks+c*128,128)]=sc
                        mx=jnp.maximum(mx,sc)
                if do_pv:
                    p=jnp.concatenate([jnp.exp2(s_scr[slot,:,pl.ds(ks+c*128,128)]-m).astype(BF) for c in range(CH//128)],axis=1)
                    acc=acc+jnp.dot(p,vv[pl.ds(ks,CH),:],preferred_element_type=F32)
        if do_pv:
            r,c,h=tile(i)
            l=acc[:,HD:]
            o_ref[pl.ds(r,R),pl.ds(c,HD)]=(acc[:,:HD]/jnp.maximum(l,1.0)).astype(BF)
            L=jnp.where(l>0,m+jnp.log2(jnp.maximum(l,1e-30)),NEG)
            lane=lax.broadcasted_iota(jnp.int32,(R,128),1)
            l_scr[pl.ds(r,R),:]=jnp.where(lax.rem(lane,8)==h,L,l_scr[pl.ds(r,R),:])
        if do_qk:
            m_scr[...]=jnp.broadcast_to(jnp.max(mx,axis=1,keepdims=True),(R,128))
    step(jnp.int32(-1),1,True,False)
    def two(t,_):
        step(2*t,0,True,True)
        step(2*t+1,1,True,True)
        return 0
    lax.fori_loop(0,NT//2-1,two,0)
    step(jnp.int32(NT-2),0,True,True)
    step(jnp.int32(NT-1),1,False,True)
    L=l_scr[...]
    hi=L.astype(BF); mid=(L-hi.astype(F32)).astype(BF); lo=(L-hi.astype(F32)-mid.astype(F32)).astype(BF)
    lane=lax.broadcasted_iota(jnp.int32,L.shape,1)
    o_ref[:,pl.ds(8*HD,128)]=jnp.where(lane<8,hi.astype(F32),jnp.where(lane<16,mid.astype(F32),jnp.where(lane<24,lo.astype(F32),0.0))).astype(BF)

def attention(pos, lim, q, k0, k1, v0, v1, nk, nv, R=256, CH=512):
    T=q.shape[0]; KEYS=k0.shape[0]; W=nk.shape[0]//2
    return pl.pallas_call(
        functools.partial(attn_kernel,R=R,CH=CH,W=W),
        out_shape=jax.ShapeDtypeStruct((T,9*HD),BF),
        in_specs=[SM]+[VM]*8,
        out_specs=VM,
        scratch_shapes=[pltpu.VMEM((2*KEYS+128,2*HD),BF),pltpu.VMEM((2*KEYS+128,2*HD),BF),
            pltpu.VMEM((2,R,2*KEYS+128),F32),pltpu.VMEM((R,128),F32),pltpu.VMEM((T,128),F32),pltpu.VMEM((T,128),jnp.int32)],
        compiler_params=pltpu.CompilerParams(vmem_limit_bytes=42*MIB),
        cost_estimate=pl.CostEstimate(flops=4*T*8*2*KEYS*HD*2,bytes_accessed=8*1024*1024,transcendentals=T*8*2*KEYS),
    )(pos,lim,q,k0,k1,v0,v1,nk,nv)


def home_kernel(recv_ref, ids_ref, idc_ref, gate_ref, att_ref, msg_ref, mat_ref):
    blocks, tok, _ = recv_ref.shape
    heads = att_ref.shape[1] // HD
    logs = []
    for s in range(blocks):
        tail = recv_ref[s, :, pl.ds(heads * HD, 128)].astype(F32)
        logs.append(tail + pltpu.roll(tail, 120, 1) + pltpu.roll(tail, 112, 1))
    top = functools.reduce(jnp.maximum, logs)
    shares = [jnp.exp2(x - top) for x in logs]
    inverse = 1.0 / functools.reduce(jnp.add, shares)
    shares = [x * inverse for x in shares]
    for h in range(heads):
        total = jnp.zeros((tok, HD), F32)
        for s in range(blocks):
            total = total + shares[s][:, h : h + 1] * recv_ref[s, :, pl.ds(h * HD, HD)].astype(F32)
        att_ref[:, pl.ds(h * HD, HD)] = total.astype(BF)
    slot = lax.broadcasted_iota(jnp.int32, (E * CAP, tok), 0)
    expert = lax.div(slot, CAP)
    member = (ids_ref[0:1, :] == expert) | (ids_ref[1:2, :] == expert)
    earlier = lax.broadcasted_iota(jnp.int32, (tok, tok), 0) < lax.broadcasted_iota(jnp.int32, (tok, tok), 1)
    rank = jnp.dot(
        jnp.where(member, 1.0, 0.0).astype(BF), jnp.where(earlier, 1.0, 0.0).astype(BF), preferred_element_type=F32
    )
    placing = member & (rank == lax.rem(slot, CAP).astype(F32))
    rows = jnp.dot(
        jnp.where(placing, 1.0, 0.0).astype(BF), att_ref[...], preferred_element_type=F32
    ).astype(BF)
    half = rows.shape[1] // 2
    for e in range(E):
        for c in range(2):
            part = rows[e * CAP : (e + 1) * CAP, c * half : (c + 1) * half]
            for y in range(msg_ref.shape[1]):
                for x in range(msg_ref.shape[3]):
                    msg_ref[e, y, c, x] = part
    gate_matrix(idc_ref, gate_ref, mat_ref, msg_ref.shape[1] * msg_ref.shape[3])


def gate_matrix(ids_ref, gate_ref, mat_ref, copies):
    tok = ids_ref.shape[0]
    terms = E * copies * CAP
    lane = lax.broadcasted_iota(jnp.int32, (tok, terms), 1)
    expert = lax.div(lane, copies * CAP)
    first, second = ids_ref[:, 0:1] == expert, ids_ref[:, 1:2] == expert
    gate = jnp.where(first, gate_ref[:, 0:1], 0.0) + jnp.where(second, gate_ref[:, 1:2], 0.0)
    earlier = lax.broadcasted_iota(jnp.int32, (tok, tok), 1) < lax.broadcasted_iota(jnp.int32, (tok, tok), 0)
    rank = jnp.dot(
        jnp.where(earlier, 1.0, 0.0).astype(BF), jnp.where(first | second, 1.0, 0.0).astype(BF), preferred_element_type=F32
    )
    gate = jnp.where(rank == lax.rem(lane, CAP).astype(F32), gate, 0.0)
    high = gate.astype(BF)
    mat_ref[pl.ds(0, tok), :] = high
    mat_ref[pl.ds(tok, tok), :] = (gate - high.astype(F32)).astype(BF)


def home(recv, ids, gates, tp):
    tok, width = recv.shape[1], recv.shape[2] - 128
    return pl.pallas_call(
        home_kernel,
        out_shape=(
            jax.ShapeDtypeStruct((tok, width), BF),
            jax.ShapeDtypeStruct((E, 2, 2, tp, CAP, width // 2), BF),
            jax.ShapeDtypeStruct((2 * tok, E * 2 * tp * CAP), BF),
        ),
        in_specs=[VM] * 4,
        out_specs=(VM, VM, VM),
        compiler_params=pltpu.CompilerParams(vmem_limit_bytes=24 * MIB),
    )(recv, ids.T, ids, gates)


def columns(x, side, half):
    return pl.ds(pl.multiple_of(x * 2 * half + side * half, half), half)


def up_part(ref, side, gain_ref, up_ref, total, square):
    seqs, tp, cap, half = ref.shape
    for x in range(tp):
        a = ref[:, x].reshape(seqs * cap, half).astype(F32)
        scaled = (a * gain_ref[:, columns(x, side, half)]).astype(BF)
        total = total + jnp.dot(scaled, up_ref[columns(x, side, half), :], preferred_element_type=F32)
        for c in range(half // 128):
            part = a[:, c * 128 : (c + 1) * 128]
            square = square + part * part
    return total, square


def up_first_kernel(core_ref, own_ref, gain_ref, up_ref, total_ref, square_ref):
    total, square = up_part(
        own_ref, core_ref[0], gain_ref, up_ref, jnp.zeros(total_ref.shape, F32), jnp.zeros(square_ref.shape, F32)
    )
    total_ref[...] = total
    square_ref[...] = square


def up_first(core, own, gain, w_up):
    rows = own.shape[0] * own.shape[2]
    return pl.pallas_call(
        up_first_kernel,
        out_shape=(
            jax.ShapeDtypeStruct((rows, w_up.shape[1]), F32),
            jax.ShapeDtypeStruct((rows, 128), F32),
        ),
        in_specs=[SM] + [VM] * 3,
        out_specs=(VM, VM),
        compiler_params=pltpu.CompilerParams(vmem_limit_bytes=24 * MIB),
        cost_estimate=pl.CostEstimate(flops=rows * own.shape[3] * 8 * w_up.shape[1], bytes_accessed=8 * MIB, transcendentals=0),
    )(core, own, gain, w_up)


def up_second_kernel(core_ref, other_ref, gain_ref, up_ref, down_ref, total_ref, square_ref, hidden_ref, send_ref):
    seqs, tp, cap, half = other_ref.shape
    other = 1 - core_ref[0]
    total, square = up_part(other_ref, other, gain_ref, up_ref, total_ref[...], square_ref[...])
    mean = jnp.sum(square, axis=1, keepdims=True) / (2 * tp * half)
    total = total * lax.rsqrt(mean + EPSILON)
    hidden = (total / (1.0 + jnp.exp(-total))).astype(BF)
    hidden_ref[...] = hidden
    for x in range(tp):
        out = jnp.dot(hidden, down_ref[:, columns(x, other, half)], preferred_element_type=F32)
        send_ref[:, x] = out.astype(BF).reshape(seqs, cap, half)


def up_second(core, other, gain, w_up, w_down, total, square):
    return pl.pallas_call(
        up_second_kernel,
        out_shape=(
            jax.ShapeDtypeStruct(total.shape, BF),
            jax.ShapeDtypeStruct(other.shape, BF),
        ),
        in_specs=[SM] + [VM] * 6,
        out_specs=(VM, VM),
        compiler_params=pltpu.CompilerParams(vmem_limit_bytes=32 * MIB),
    )(core, other, gain, w_up, w_down, total, square)


def down_kernel(core_ref, hidden_ref, down_ref, partner_ref, out_ref):
    seqs, tp, cap, half = out_ref.shape
    hidden = hidden_ref[...]
    for x in range(tp):
        out = jnp.dot(hidden, down_ref[:, columns(x, core_ref[0], half)], preferred_element_type=F32)
        out = out + partner_ref[:, x].reshape(seqs * cap, half).astype(F32)
        out_ref[:, x] = out.astype(BF).reshape(seqs, cap, half)


def down_project(core, hidden, w_down, partner):
    return pl.pallas_call(
        down_kernel,
        out_shape=jax.ShapeDtypeStruct(partner.shape, BF),
        in_specs=[SM] + [VM] * 3,
        out_specs=VM,
        compiler_params=pltpu.CompilerParams(vmem_limit_bytes=24 * MIB),
    )(core, hidden, w_down, partner)


def mix_kernel(recv_ref, mat_ref, out_ref):
    experts, pair, cores, tp, cap, half = recv_ref.shape
    tok = out_ref.shape[0]
    for c in range(cores):
        values = recv_ref[:, :, c].reshape(experts * pair * tp * cap, half)
        out = jnp.dot(mat_ref[...], values, preferred_element_type=F32)
        out_ref[:, pl.ds(c * half, half)] = (out[:tok] + out[tok:]).astype(BF)


def mix(recv, matrix):
    return pl.pallas_call(
        mix_kernel,
        out_shape=jax.ShapeDtypeStruct((matrix.shape[0] // 2, 2 * recv.shape[5]), BF),
        in_specs=[VM] * 2,
        out_specs=VM,
        compiler_params=pltpu.CompilerParams(vmem_limit_bytes=24 * MIB),
    )(recv, matrix)


def per_device(
    queries, cache_keys, cache_values, new_keys, new_values, reach, norm_gain, gate_weights, expert_ids, w_up, w_down
):
    seqs, tp = lax.axis_size("seq"), lax.axis_size("tp")
    seq = lax.axis_index("seq")
    core = lax.rem(seq, 2)
    partner = seq + 1 - 2 * core
    tok, width = queries.shape
    ctx = cache_keys.shape[0]
    chips = seqs // 2
    same_core = [list(range(c, seqs, 2)) for c in range(2)]
    swap = [(i, i ^ 1) for i in range(seqs)]

    def swapped(value):
        return lax.ppermute(value, "seq", swap)

    other_keys, other_values = swapped(cache_keys), swapped(cache_values)
    other_new_keys, other_new_values = swapped(new_keys), swapped(new_values)
    all_queries = lax.all_to_all(
        jnp.broadcast_to(queries[None], (chips, tok, width)),
        "seq", 0, 0, axis_index_groups=same_core, tiled=True,
    ).reshape(chips * tok, width)
    limits = lax.dynamic_index_in_dim(reach.reshape(chips, 2, tok), core, 1, keepdims=False)
    limits = limits.reshape(1, chips * tok)
    places = jnp.stack([seq * ctx, partner * ctx, seq * tok, partner * tok, core]).astype(jnp.int32)
    outs = attention(
        places, limits, all_queries, cache_keys, other_keys, cache_values, other_values,
        jnp.concatenate([new_keys, other_new_keys], axis=0),
        jnp.concatenate([new_values, other_new_values], axis=0),
    )
    arrived = lax.all_to_all(
        outs.reshape(chips, tok, outs.shape[1]), "seq", 0, 0, axis_index_groups=same_core, tiled=True
    )
    attended, message, matrix = home(arrived, expert_ids, gate_weights, tp)
    half = width // 2
    rows = lax.all_to_all(
        message.reshape(seqs * tp, CAP, half), ("seq", "tp"), 0, 0, tiled=True
    ).reshape(seqs, tp, CAP, half)
    side = core.astype(jnp.int32).reshape(1)
    gain = norm_gain.reshape(1, -1)
    total, square = up_first(side, rows, gain, w_up[0])
    hidden, send = up_second(side, swapped(rows), gain, w_up[0], w_down[0], total, square)
    result = down_project(side, hidden, w_down[0], swapped(send))
    returned = lax.all_to_all(
        result.reshape(seqs * tp, CAP, half), ("seq", "tp"), 0, 0, tiled=True
    ).reshape(E, 2, 2, tp, CAP, half)
    return attended, mix(returned, matrix)


def solution(mesh):
    placed = (
        P("seq", "tp"),
        P("seq", "tp"),
        P("seq", "tp"),
        P("seq", "tp"),
        P("seq", "tp"),
        P(),
        P(),
        P("seq", None),
        P("seq", None),
        P("seq", None, "tp"),
        P("seq", "tp", None),
    )
    return jax.shard_map(
        per_device,
        mesh=mesh,
        in_specs=placed,
        out_specs=(P("seq", "tp"), P("seq", "tp")),
        check_vma=False,
    )
```

```python
import functools
import math

import jax
import jax.numpy as jnp
from jax import lax
from jax.experimental import pallas as pl
from jax.experimental.pallas import tpu as pltpu
from jax.sharding import PartitionSpec as P

HD = 128
E = 8
CAP = 16
EPSILON = 1e-05
NEG = -1e30
FLOOR = -1e20
BF = jnp.bfloat16
F32 = jnp.float32
SCALE = HD**-0.5 * math.log2(math.e)
MIB = 1024 * 1024
VM = pl.BlockSpec(memory_space=pltpu.VMEM)
SM = pl.BlockSpec(memory_space=pltpu.SMEM)
HBM = pl.BlockSpec(memory_space=pltpu.HBM)

def attn_kernel(pos_ref, reach_ref, q_ref, kk, vv, o_ref, s_scr, m_scr, l_scr, lim_ref, *, R, CH, W):
    T=q_ref.shape[0]; KEYS=(kk.shape[0]-128)//2; NT=(T//R)*8; NCH=KEYS//CH; WIN=2*KEYS
    l_scr[...]=jnp.zeros_like(l_scr)
    for t in range(T//R):
        lim_ref[pl.ds(t*R,R),:]=jnp.transpose(jnp.broadcast_to(reach_ref[:,pl.ds(t*R,R)],(128,R)))
    def tile(i):
        h=lax.rem(i,8); tb=lax.div(i,8)
        return pl.multiple_of(tb*R,R), pl.multiple_of(h*HD,HD), h
    def load_q(i):
        r,c,_=tile(i)
        qf=q_ref[pl.ds(r,R),pl.ds(c,HD)].astype(F32)*SCALE
        hi=qf.astype(BF); lo=(qf-hi.astype(F32)).astype(BF)
        return jnp.concatenate([hi,lo],axis=1)
    def dotk(qq,k):
        return lax.dot_general(qq,k,(((1,),(1,)),((),())),preferred_element_type=F32)
    def window_scores(i, qq):
        r,_,_=tile(i)
        s=dotk(qq,kk[pl.ds(WIN,128),:])
        lane=lax.broadcasted_iota(jnp.int32,(R,128),1)
        row=lax.broadcasted_iota(jnp.int32,(R,128),0)+r
        tok=lax.div(row,W)*(2*W)+lax.rem(row,W)+pos_ref[4]*W
        key=jnp.where(lane<W,lane+pos_ref[2],lane-W+pos_ref[3])
        return jnp.where((lane<2*W)&(key<=tok),s,NEG)
    def step(i, slot, do_qk, do_pv):
        if do_qk:
            qq=load_q(i+1)
            r1,_,_=tile(i+1)
            lim=lim_ref[pl.ds(r1,R),:]
            lane0=lax.broadcasted_iota(jnp.int32,(R,128),1)
            mx=jnp.full((R,128),FLOOR,F32)
            sw=window_scores(i+1,qq)
            s_scr[1-slot,:,pl.ds(WIN,128)]=sw
            mx=jnp.maximum(mx,sw)
        if do_pv:
            m=m_scr[...]
            p=jnp.exp2(s_scr[slot,:,pl.ds(WIN,128)]-m)
            acc=jnp.dot(p.astype(BF),vv[pl.ds(WIN,128),:],preferred_element_type=F32)
        for half in range(2):
            if do_qk:
                limh=lim-pos_ref[half]
            for j in range(NCH):
                ks=half*KEYS+j*CH
                if do_qk:
                    s=dotk(qq,kk[pl.ds(ks,CH),:])
                    for c in range(CH//128):
                        sc=jnp.where(lane0+(j*CH+c*128)<limh,s[:,c*128:(c+1)*128],NEG)
                        s_scr[1-slot,:,pl.ds(ks+c*128,128)]=sc
                        mx=jnp.maximum(mx,sc)
                if do_pv:
                    p=jnp.concatenate([jnp.exp2(s_scr[slot,:,pl.ds(ks+c*128,128)]-m).astype(BF) for c in range(CH//128)],axis=1)
                    acc=acc+jnp.dot(p,vv[pl.ds(ks,CH),:],preferred_element_type=F32)
        if do_pv:
            r,c,h=tile(i)
            l=acc[:,HD:]
            o_ref[pl.ds(r,R),pl.ds(c,HD)]=(acc[:,:HD]/jnp.maximum(l,1.0)).astype(BF)
            L=jnp.where(l>0,m+jnp.log2(jnp.maximum(l,1e-30)),NEG)
            lane=lax.broadcasted_iota(jnp.int32,(R,128),1)
            l_scr[pl.ds(r,R),:]=jnp.where(lax.rem(lane,8)==h,L,l_scr[pl.ds(r,R),:])
        if do_qk:
            m_scr[...]=jnp.broadcast_to(jnp.max(mx,axis=1,keepdims=True),(R,128))
    step(jnp.int32(-1),1,True,False)
    def two(t,_):
        step(2*t,0,True,True)
        step(2*t+1,1,True,True)
        return 0
    lax.fori_loop(0,NT//2-1,two,0)
    step(jnp.int32(NT-2),0,True,True)
    step(jnp.int32(NT-1),1,False,True)
    L=l_scr[...]
    hi=L.astype(BF); mid=(L-hi.astype(F32)).astype(BF); lo=(L-hi.astype(F32)-mid.astype(F32)).astype(BF)
    lane=lax.broadcasted_iota(jnp.int32,L.shape,1)
    o_ref[:,pl.ds(8*HD,128)]=jnp.where(lane<8,hi.astype(F32),jnp.where(lane<16,mid.astype(F32),jnp.where(lane<24,lo.astype(F32),0.0))).astype(BF)

def attention(pos, reach, q, kk, vv, W, R=256, CH=512):
    T=q.shape[0]; keys=kk.shape[0]
    return pl.pallas_call(
        functools.partial(attn_kernel,R=R,CH=CH,W=W),
        out_shape=jax.ShapeDtypeStruct((T,9*HD),BF),
        in_specs=[SM]+[VM]*4,
        out_specs=VM,
        scratch_shapes=[pltpu.VMEM((2,R,keys),F32),pltpu.VMEM((R,128),F32),pltpu.VMEM((T,128),F32),pltpu.VMEM((T,128),jnp.int32)],
        compiler_params=pltpu.CompilerParams(vmem_limit_bytes=36*MIB),
        cost_estimate=pl.CostEstimate(flops=32*T*keys*HD,bytes_accessed=8*MIB,transcendentals=T*8*keys),
    )(pos,reach,q,kk,vv)


def tables_kernel(k0_ref, k1_ref, v0_ref, v1_ref, nk0_ref, nk1_ref, nv0_ref, nv1_ref, kk_ref, vv_ref):
    first = 0
    for keys, values in ((k0_ref, v0_ref), (k1_ref, v1_ref), (nk0_ref, nv0_ref), (nk1_ref, nv1_ref)):
        count = keys.shape[0]
        rows = pl.ds(first, count)
        kk_ref[rows, pl.ds(0, HD)] = keys[...]
        kk_ref[rows, pl.ds(HD, HD)] = keys[...]
        vv_ref[rows, pl.ds(0, HD)] = values[...]
        vv_ref[rows, pl.ds(HD, HD)] = jnp.ones((count, HD), BF)
        first += count
    rest = kk_ref.shape[0] - first
    kk_ref[pl.ds(first, rest), :] = jnp.zeros((rest, 2 * HD), BF)
    vv_ref[pl.ds(first, rest), :] = jnp.zeros((rest, 2 * HD), BF)


def tables(*rows):
    keys = 2 * rows[0].shape[0] + 128
    shape = jax.ShapeDtypeStruct((keys, 2 * HD), BF)
    return pl.pallas_call(
        tables_kernel,
        out_shape=(shape, shape),
        in_specs=[VM] * 8,
        out_specs=(VM, VM),
        compiler_params=pltpu.CompilerParams(vmem_limit_bytes=20 * MIB),
        cost_estimate=pl.CostEstimate(flops=0, bytes_accessed=12 * MIB, transcendentals=0),
    )(*rows)


def home_kernel(recv_ref, ids_ref, gate_ref, att_ref, msg_ref, mat_ref):
    blocks, tok, _ = recv_ref.shape
    heads = att_ref.shape[1] // HD
    logs = []
    for s in range(blocks):
        tail = recv_ref[s, :, pl.ds(heads * HD, 128)].astype(F32)
        logs.append(tail + pltpu.roll(tail, 120, 1) + pltpu.roll(tail, 112, 1))
    top = functools.reduce(jnp.maximum, logs)
    shares = [jnp.exp2(x - top) for x in logs]
    inverse = 1.0 / functools.reduce(jnp.add, shares)
    shares = [x * inverse for x in shares]
    for h in range(heads):
        total = jnp.zeros((tok, HD), F32)
        for s in range(blocks):
            total = total + shares[s][:, h : h + 1] * recv_ref[s, :, pl.ds(h * HD, HD)].astype(F32)
        att_ref[:, pl.ds(h * HD, HD)] = total.astype(BF)
    slot = lax.broadcasted_iota(jnp.int32, (E * CAP, tok), 0)
    expert = lax.div(slot, CAP)
    member = (ids_ref[0:1, :] == expert) | (ids_ref[1:2, :] == expert)
    earlier = lax.broadcasted_iota(jnp.int32, (tok, tok), 0) < lax.broadcasted_iota(jnp.int32, (tok, tok), 1)
    rank = jnp.dot(
        jnp.where(member, 1.0, 0.0).astype(BF), jnp.where(earlier, 1.0, 0.0).astype(BF), preferred_element_type=F32
    )
    placing = member & (rank == lax.rem(slot, CAP).astype(F32))
    rows = jnp.dot(
        jnp.where(placing, 1.0, 0.0).astype(BF), att_ref[...], preferred_element_type=F32
    ).astype(BF)
    half = rows.shape[1] // 2
    for e in range(E):
        for c in range(2):
            part = rows[e * CAP : (e + 1) * CAP, c * half : (c + 1) * half]
            for y in range(msg_ref.shape[1]):
                for x in range(msg_ref.shape[3]):
                    msg_ref[e, y, c, x] = part
    gate_matrix(ids_ref, gate_ref, mat_ref, msg_ref.shape[1] * msg_ref.shape[3])


def gate_matrix(ids_ref, gate_ref, mat_ref, copies):
    tok = ids_ref.shape[1]
    terms = E * copies * CAP
    same = lax.broadcasted_iota(jnp.int32, (tok, tok), 0) == lax.broadcasted_iota(jnp.int32, (tok, tok), 1)

    def column(ref, k):
        row = jnp.broadcast_to(ref[k : k + 1, :], (tok, tok))
        return jnp.sum(jnp.where(same, row, jnp.zeros_like(row)), axis=1, keepdims=True)

    lane = lax.broadcasted_iota(jnp.int32, (tok, terms), 1)
    expert = lax.div(lane, copies * CAP)
    first, second = column(ids_ref, 0) == expert, column(ids_ref, 1) == expert
    gate = jnp.where(first, column(gate_ref, 0), 0.0) + jnp.where(second, column(gate_ref, 1), 0.0)
    earlier = lax.broadcasted_iota(jnp.int32, (tok, tok), 1) < lax.broadcasted_iota(jnp.int32, (tok, tok), 0)
    rank = jnp.dot(
        jnp.where(earlier, 1.0, 0.0).astype(BF), jnp.where(first | second, 1.0, 0.0).astype(BF), preferred_element_type=F32
    )
    gate = jnp.where(rank == lax.rem(lane, CAP).astype(F32), gate, 0.0)
    high = gate.astype(BF)
    mat_ref[pl.ds(0, tok), :] = high
    mat_ref[pl.ds(tok, tok), :] = (gate - high.astype(F32)).astype(BF)


def home(recv, ids, gates, tp):
    tok, width = recv.shape[1], recv.shape[2] - 128
    return pl.pallas_call(
        home_kernel,
        out_shape=(
            jax.ShapeDtypeStruct((tok, width), BF),
            jax.ShapeDtypeStruct((E, 2, 2, tp, CAP, width // 2), BF),
            jax.ShapeDtypeStruct((2 * tok, E * 2 * tp * CAP), BF),
        ),
        in_specs=[VM] * 3,
        out_specs=(VM, VM, VM),
        compiler_params=pltpu.CompilerParams(vmem_limit_bytes=24 * MIB),
    )(recv, ids.T, gates.T)


def columns(x, side, half):
    return pl.ds(pl.multiple_of(x * 2 * half + side * half, half), half)


def up_part(ref, side, gain_ref, up_ref, w_buf, sems, total, square):
    seqs, tp, cap, half = ref.shape
    copies = [pltpu.make_async_copy(up_ref.at[columns(x, side, half), :], w_buf.at[x], sems.at[x]) for x in range(tp)]
    for copy in copies:
        copy.start()
    for x in range(tp):
        a = ref[:, x].reshape(seqs * cap, half).astype(F32)
        scaled = (a * gain_ref[:, columns(x, side, half)]).astype(BF)
        for c in range(half // 128):
            part = a[:, c * 128 : (c + 1) * 128]
            square = square + part * part
        copies[x].wait()
        total = total + jnp.dot(scaled, w_buf[x], preferred_element_type=F32)
    return total, square


def up_first_kernel(core_ref, own_ref, gain_ref, up_ref, total_ref, square_ref, w_buf, sems):
    total, square = up_part(
        own_ref, core_ref[0], gain_ref, up_ref, w_buf, sems, jnp.zeros(total_ref.shape, F32), jnp.zeros(square_ref.shape, F32)
    )
    total_ref[...] = total
    square_ref[...] = square


def up_first(core, own, gain, w_up):
    rows, tp, half, hid = own.shape[0] * own.shape[2], own.shape[1], own.shape[3], w_up.shape[1]
    return pl.pallas_call(
        up_first_kernel,
        out_shape=(
            jax.ShapeDtypeStruct((rows, hid), F32),
            jax.ShapeDtypeStruct((rows, 128), F32),
        ),
        in_specs=[SM, VM, VM, HBM],
        out_specs=(VM, VM),
        scratch_shapes=[pltpu.VMEM((tp, half, hid), BF), pltpu.SemaphoreType.DMA((tp,))],
        compiler_params=pltpu.CompilerParams(vmem_limit_bytes=24 * MIB),
        cost_estimate=pl.CostEstimate(flops=2 * rows * tp * half * hid, bytes_accessed=5 * MIB, transcendentals=0),
    )(core, own, gain, w_up)


def up_second_kernel(
    core_ref, other_ref, gain_ref, up_ref, down_ref, total_ref, square_ref, hidden_ref, send_ref, w_buf, d_buf, sems
):
    seqs, tp, cap, half = other_ref.shape
    other = 1 - core_ref[0]
    copies = [pltpu.make_async_copy(down_ref.at[:, columns(x, other, half)], d_buf.at[x], sems.at[tp + x]) for x in range(tp)]
    for copy in copies:
        copy.start()
    total, square = up_part(other_ref, other, gain_ref, up_ref, w_buf, sems, total_ref[...], square_ref[...])
    mean = jnp.sum(square, axis=1, keepdims=True) / (2 * tp * half)
    total = total * lax.rsqrt(mean + EPSILON)
    hidden = (total / (1.0 + jnp.exp(-total))).astype(BF)
    hidden_ref[...] = hidden
    for x in range(tp):
        copies[x].wait()
        out = jnp.dot(hidden, d_buf[x], preferred_element_type=F32)
        send_ref[:, x] = out.astype(BF).reshape(seqs, cap, half)


def up_second(core, other, gain, w_up, w_down, total, square):
    tp, half, hid = other.shape[1], other.shape[3], w_up.shape[1]
    return pl.pallas_call(
        up_second_kernel,
        out_shape=(
            jax.ShapeDtypeStruct(total.shape, BF),
            jax.ShapeDtypeStruct(other.shape, BF),
        ),
        in_specs=[SM, VM, VM, HBM, HBM, VM, VM],
        out_specs=(VM, VM),
        scratch_shapes=[
            pltpu.VMEM((tp, half, hid), BF),
            pltpu.VMEM((tp, hid, half), BF),
            pltpu.SemaphoreType.DMA((2 * tp,)),
        ],
        compiler_params=pltpu.CompilerParams(vmem_limit_bytes=28 * MIB),
    )(core, other, gain, w_up, w_down, total, square)


def down_kernel(core_ref, hidden_ref, down_ref, out_ref, d_buf, sems):
    seqs, tp, cap, half = out_ref.shape
    copies = [
        pltpu.make_async_copy(down_ref.at[:, columns(x, core_ref[0], half)], d_buf.at[x], sems.at[x]) for x in range(tp)
    ]
    for copy in copies:
        copy.start()
    hidden = hidden_ref[...]
    for x in range(tp):
        copies[x].wait()
        out_ref[:, x] = jnp.dot(hidden, d_buf[x], preferred_element_type=F32).reshape(seqs, cap, half)


def down_project(core, hidden, w_down, shape):
    tp, half, hid = shape[1], shape[3], hidden.shape[1]
    return pl.pallas_call(
        down_kernel,
        out_shape=jax.ShapeDtypeStruct(shape, F32),
        in_specs=[SM, VM, HBM],
        out_specs=VM,
        scratch_shapes=[pltpu.VMEM((tp, hid, half), BF), pltpu.SemaphoreType.DMA((tp,))],
        compiler_params=pltpu.CompilerParams(vmem_limit_bytes=24 * MIB),
        cost_estimate=pl.CostEstimate(flops=2 * hidden.shape[0] * tp * half * hid, bytes_accessed=5 * MIB, transcendentals=0),
    )(core, hidden, w_down)


def join_kernel(keep_ref, partner_ref, out_ref):
    for x in range(out_ref.shape[1]):
        out_ref[:, x] = (keep_ref[:, x] + partner_ref[:, x].astype(F32)).astype(BF)


def join(keep, partner):
    return pl.pallas_call(
        join_kernel,
        out_shape=jax.ShapeDtypeStruct(partner.shape, BF),
        in_specs=[VM] * 2,
        out_specs=VM,
        compiler_params=pltpu.CompilerParams(vmem_limit_bytes=16 * MIB),
    )(keep, partner)


def mix_kernel(recv_ref, mat_ref, out_ref):
    experts, pair, cores, tp, cap, half = recv_ref.shape
    tok = out_ref.shape[0]
    for c in range(cores):
        values = recv_ref[:, :, c].reshape(experts * pair * tp * cap, half)
        out = jnp.dot(mat_ref[...], values, preferred_element_type=F32)
        out_ref[:, pl.ds(c * half, half)] = (out[:tok] + out[tok:]).astype(BF)


def mix(recv, matrix):
    return pl.pallas_call(
        mix_kernel,
        out_shape=jax.ShapeDtypeStruct((matrix.shape[0] // 2, 2 * recv.shape[5]), BF),
        in_specs=[VM] * 2,
        out_specs=VM,
        compiler_params=pltpu.CompilerParams(vmem_limit_bytes=24 * MIB),
    )(recv, matrix)


def per_device(
    queries, cache_keys, cache_values, new_keys, new_values, reach, norm_gain, gate_weights, expert_ids, w_up, w_down
):
    seqs, tp = lax.axis_size("seq"), lax.axis_size("tp")
    seq = lax.axis_index("seq")
    core = lax.rem(seq, 2)
    partner = seq + 1 - 2 * core
    tok, width = queries.shape
    ctx = cache_keys.shape[0]
    chips = seqs // 2
    same_core = [list(range(c, seqs, 2)) for c in range(2)]
    swap = [(i, i ^ 1) for i in range(seqs)]

    def swapped(value):
        return lax.ppermute(value, "seq", swap)

    other_keys, other_values = swapped(cache_keys), swapped(cache_values)
    other_new_keys, other_new_values = swapped(new_keys), swapped(new_values)
    all_queries = lax.all_to_all(
        jnp.broadcast_to(queries[None], (chips, tok, width)),
        "seq", 0, 0, axis_index_groups=same_core, tiled=True,
    ).reshape(chips * tok, width)
    limits = lax.dynamic_index_in_dim(reach.reshape(chips, 2, tok), core, 1, keepdims=False)
    limits = limits.reshape(1, chips * tok)
    places = jnp.stack([seq * ctx, partner * ctx, seq * tok, partner * tok, core]).astype(jnp.int32)
    kk, vv = tables(
        cache_keys, other_keys, cache_values, other_values, new_keys, other_new_keys, new_values, other_new_values
    )
    outs = attention(places, limits, all_queries, kk, vv, tok)
    arrived = lax.all_to_all(
        outs.reshape(chips, tok, outs.shape[1]), "seq", 0, 0, axis_index_groups=same_core, tiled=True
    )
    attended, message, matrix = home(arrived, expert_ids, gate_weights, tp)
    half = width // 2
    rows = lax.all_to_all(
        message.reshape(seqs * tp, CAP, half), ("seq", "tp"), 0, 0, tiled=True
    ).reshape(seqs, tp, CAP, half)
    side = core.astype(jnp.int32).reshape(1)
    gain = norm_gain.reshape(1, -1)
    up_rows = pltpu.with_memory_space_constraint(w_up[0], pltpu.HBM)
    down_rows = pltpu.with_memory_space_constraint(w_down[0], pltpu.HBM)
    total, square = up_first(side, rows, gain, up_rows)
    hidden, send = up_second(side, swapped(rows), gain, up_rows, down_rows, total, square)
    result = join(down_project(side, hidden, down_rows, send.shape), swapped(send))
    returned = lax.all_to_all(
        result.reshape(seqs * tp, CAP, half), ("seq", "tp"), 0, 0, tiled=True
    ).reshape(E, 2, 2, tp, CAP, half)
    return attended, mix(returned, matrix)


def solution(mesh):
    placed = (
        P("seq", "tp"),
        P("seq", "tp"),
        P("seq", "tp"),
        P("seq", "tp"),
        P("seq", "tp"),
        P(),
        P(),
        P("seq", None),
        P("seq", None),
        P("seq", None, "tp"),
        P("seq", "tp", None),
    )
    return jax.shard_map(
        per_device,
        mesh=mesh,
        in_specs=placed,
        out_specs=(P("seq", "tp"), P("seq", "tp")),
        check_vma=False,
    )
```

```python
import functools
import math

import jax
import jax.numpy as jnp
from jax import lax
from jax.experimental import pallas as pl
from jax.experimental.pallas import tpu as pltpu
from jax.sharding import PartitionSpec as P

HD = 128
E = 8
CAP = 16
EPSILON = 1e-05
NEG = -1e30
FLOOR = -1e20
BF = jnp.bfloat16
F32 = jnp.float32
SCALE = HD**-0.5 * math.log2(math.e)
MIB = 1024 * 1024
VM = pl.BlockSpec(memory_space=pltpu.VMEM)
HBM = pl.BlockSpec(memory_space=pltpu.HBM)

def attn_kernel(*refs, parts, earlier, CH):
    reach_ref = refs[0]
    q_refs, refs = refs[1 : 1 + parts], refs[1 + parts :]
    (k0_ref, v0_ref, k1_ref, v1_ref, n0_ref, n1_ref), refs = refs[:6], refs[6:]
    if earlier:
        prev_ref, refs = refs[0], refs[1:]
    o_ref, q_all, kk, vv, k_own, v_own, s_scr, m_scr, l_scr, lim_ref, tok_ref, sems = refs
    copies = [pltpu.make_async_copy(k0_ref, k_own, sems.at[0]), pltpu.make_async_copy(v0_ref, v_own, sems.at[1])]
    for copy in copies:
        copy.start(priority=1)
    tokens = q_refs[0].shape[0]
    W = n0_ref.shape[0] // 2
    blocks = tokens // W
    T = parts * tokens
    KEYS = k_own.shape[0]
    WIN = 2 * KEYS
    NCH = KEYS // CH
    R = 2 * tokens
    NT = parts * 4
    side = blocks
    seq = lax.axis_index("seq")
    core = lax.rem(seq, 2)
    partner = seq + 1 - 2 * core
    z, y = lax.div(seq, 2 * side), lax.rem(lax.div(seq, 2), side)

    def block(b):
        return lax.rem(z + b // side, side) * side + lax.rem(y + b % side, side)

    def fill(rows, keys, values):
        kk[rows, pl.ds(0, HD)] = keys
        kk[rows, pl.ds(HD, HD)] = keys
        vv[rows, pl.ds(0, HD)] = values
        vv[rows, pl.ds(HD, HD)] = jnp.ones_like(values)

    for p in range(parts):
        rows = pl.ds(p * tokens, tokens)
        q_all[rows, :] = q_refs[p][...]
        lim_ref[rows, :] = jnp.transpose(jnp.broadcast_to(reach_ref[:, p * tokens : (p + 1) * tokens], (128, tokens)))
    for b in range(T // W):
        tok_ref[pl.ds(b * W, W), :] = lax.broadcasted_iota(jnp.int32, (W, 128), 0) + (
            block(b + blocks * earlier) * 2 + core
        ) * W
    l_scr[...] = jnp.zeros_like(l_scr)
    if earlier:
        for b in range(blocks):
            o_ref[pl.ds(pl.multiple_of(block(b) * W, W), W), :] = prev_ref[pl.ds(b * W, W), :]
    fill(pl.ds(KEYS, KEYS), k1_ref[...], v1_ref[...])
    fill(pl.ds(WIN, W), n0_ref[pl.ds(0, W), :], n0_ref[pl.ds(W, W), :])
    fill(pl.ds(WIN + W, W), n1_ref[pl.ds(0, W), :], n1_ref[pl.ds(W, W), :])
    rest = pl.ds(WIN + 2 * W, 128 - 2 * W)
    fill(rest, jnp.zeros((128 - 2 * W, HD), BF), jnp.zeros((128 - 2 * W, HD), BF))
    for copy in copies:
        copy.wait()
    fill(pl.ds(0, KEYS), k_own[...], v_own[...])

    def target(i, b):
        if not earlier:
            return pl.multiple_of((lax.div(i, 4) * blocks + b) * W, W)
        place = lax.rem(z + lax.div(i, 4) + 1, side) * side + lax.rem(y + b, side)
        return pl.multiple_of(place * W, W)

    def tile(i):
        return pl.multiple_of(lax.div(i, 4) * tokens, tokens), lax.rem(i, 4) * 2

    def twice(x):
        return jnp.concatenate([x, x], axis=0)

    def load_q(i):
        r, h = tile(i)
        out = []
        for k in range(2):
            qf = q_all[pl.ds(r, tokens), pl.ds(pl.multiple_of((h + k) * HD, HD), HD)].astype(F32) * SCALE
            hi = qf.astype(BF)
            out.append(jnp.concatenate([hi, (qf - hi.astype(F32)).astype(BF)], axis=1))
        return jnp.concatenate(out, axis=0)

    def dotk(qq, k):
        return lax.dot_general(qq, k, (((1,), (1,)), ((), ())), preferred_element_type=F32)

    def window_scores(i, qq):
        r, _ = tile(i)
        s = dotk(qq, kk[pl.ds(WIN, 128), :])
        lane = lax.broadcasted_iota(jnp.int32, (R, 128), 1)
        key = jnp.where(lane < W, lane + seq * W, lane - W + partner * W)
        return jnp.where((lane < 2 * W) & (key <= twice(tok_ref[pl.ds(r, tokens), :])), s, NEG)

    def step(i, do_qk, do_pv):
        if do_qk:
            qq = load_q(i + 1)
            r1, _ = tile(i + 1)
            lim = twice(lim_ref[pl.ds(r1, tokens), :])
            lane0 = lax.broadcasted_iota(jnp.int32, (R, 128), 1)
            sw = window_scores(i + 1, qq)
            mx = jnp.maximum(sw, FLOOR)
        if do_pv:
            m = m_scr[...]
            p = jnp.exp2(s_scr[:, pl.ds(WIN, 128)] - m)
            acc = jnp.dot(p.astype(BF), vv[pl.ds(WIN, 128), :], preferred_element_type=F32)
        if do_qk:
            s_scr[:, pl.ds(WIN, 128)] = sw
        for half in range(2):
            if do_qk:
                limh = lim - (seq, partner)[half] * KEYS
            for j in range(NCH):
                ks = half * KEYS + j * CH
                if do_pv:
                    p = jnp.concatenate(
                        [jnp.exp2(s_scr[:, pl.ds(ks + c * 128, 128)] - m).astype(BF) for c in range(CH // 128)], axis=1
                    )
                    acc = acc + jnp.dot(p, vv[pl.ds(ks, CH), :], preferred_element_type=F32)
                if do_qk:
                    s = dotk(qq, kk[pl.ds(ks, CH), :])
                    for c in range(CH // 128):
                        sc = jnp.where(lane0 + (j * CH + c * 128) < limh, s[:, c * 128 : (c + 1) * 128], NEG)
                        s_scr[:, pl.ds(ks + c * 128, 128)] = sc
                        mx = jnp.maximum(mx, sc)
        if do_pv:
            r, h = tile(i)
            l = acc[:, HD:]
            out = (acc[:, :HD] / jnp.maximum(l, 1.0)).astype(BF)
            L = jnp.where(l > 0, m + jnp.log2(jnp.maximum(l, 1e-30)), NEG)
            lane = lax.rem(lax.broadcasted_iota(jnp.int32, (tokens, 128), 1), 8)
            old = l_scr[pl.ds(r, tokens), :]
            for k in range(2):
                old = jnp.where(lane == h + k, L[k * tokens : (k + 1) * tokens], old)
                cols = pl.ds(pl.multiple_of((h + k) * HD, HD), HD)
                for b in range(blocks):
                    o_ref[pl.ds(target(i, b), W), cols] = out[k * tokens + b * W : k * tokens + (b + 1) * W]
            l_scr[pl.ds(r, tokens), :] = old
        if do_qk:
            m_scr[...] = jnp.broadcast_to(jnp.max(mx, axis=1, keepdims=True), (R, 128))

    step(jnp.int32(-1), True, False)

    def both(i, _):
        step(i, True, True)
        return 0

    lax.fori_loop(0, NT - 1, both, 0)
    step(jnp.int32(NT - 1), False, True)
    L = l_scr[...]
    hi = L.astype(BF).astype(F32)
    mid = (L - hi).astype(BF).astype(F32)
    lane = lax.broadcasted_iota(jnp.int32, L.shape, 1)
    packed = jnp.where(lane < 8, hi, jnp.where(lane < 16, mid, jnp.where(lane < 24, L - hi - mid, 0.0))).astype(BF)
    for b in range(T // W):
        place = block(b + blocks) if earlier else b
        o_ref[pl.ds(pl.multiple_of(place * W, W), W), pl.ds(8 * HD, 128)] = packed[b * W : (b + 1) * W]


def attention(reach, qs, tables, prev=None, CH=512):
    tokens = qs[0].shape[0]
    T = len(qs) * tokens
    keys = 2 * tables[0].shape[0] + 128
    rows = T + (0 if prev is None else tokens)
    more = () if prev is None else (prev,)
    return pl.pallas_call(
        functools.partial(attn_kernel, parts=len(qs), earlier=prev is not None, CH=CH),
        out_shape=jax.ShapeDtypeStruct((rows, 9 * HD), BF),
        in_specs=[VM] * (1 + len(qs)) + [HBM] * 2 + [VM] * (4 + len(more)),
        out_specs=VM,
        scratch_shapes=[
            pltpu.VMEM((T, 8 * HD), BF),
            pltpu.VMEM((keys, 2 * HD), BF),
            pltpu.VMEM((keys, 2 * HD), BF),
            pltpu.VMEM(tables[0].shape, BF),
            pltpu.VMEM(tables[0].shape, BF),
            pltpu.VMEM((2 * tokens, keys), F32),
            pltpu.VMEM((2 * tokens, 128), F32),
            pltpu.VMEM((T, 128), F32),
            pltpu.VMEM((T, 128), jnp.int32),
            pltpu.VMEM((T, 128), jnp.int32),
            pltpu.SemaphoreType.DMA((2,)),
        ],
        compiler_params=pltpu.CompilerParams(vmem_limit_bytes=36 * MIB),
        cost_estimate=pl.CostEstimate(flops=32 * T * keys * HD, bytes_accessed=8 * MIB, transcendentals=T * 8 * keys),
    )(reach, *qs, *tables, *more)


def home_kernel(recv_ref, ids_ref, gate_ref, att_ref, msg_ref, mat_ref):
    blocks, tok, _ = recv_ref.shape
    heads = att_ref.shape[1] // HD
    logs = []
    for s in range(blocks):
        tail = recv_ref[s, :, pl.ds(heads * HD, 128)].astype(F32)
        logs.append(tail + pltpu.roll(tail, 120, 1) + pltpu.roll(tail, 112, 1))
    top = functools.reduce(jnp.maximum, logs)
    shares = [jnp.exp2(x - top) for x in logs]
    inverse = 1.0 / functools.reduce(jnp.add, shares)
    shares = [x * inverse for x in shares]
    for h in range(heads):
        total = jnp.zeros((tok, HD), F32)
        for s in range(blocks):
            total = total + shares[s][:, h : h + 1] * recv_ref[s, :, pl.ds(h * HD, HD)].astype(F32)
        att_ref[:, pl.ds(h * HD, HD)] = total.astype(BF)
    slot = lax.broadcasted_iota(jnp.int32, (E * CAP, tok), 0)
    expert = lax.div(slot, CAP)
    member = (ids_ref[0:1, :] == expert) | (ids_ref[1:2, :] == expert)
    earlier = lax.broadcasted_iota(jnp.int32, (tok, tok), 0) < lax.broadcasted_iota(jnp.int32, (tok, tok), 1)
    rank = jnp.dot(
        jnp.where(member, 1.0, 0.0).astype(BF), jnp.where(earlier, 1.0, 0.0).astype(BF), preferred_element_type=F32
    )
    placing = member & (rank == lax.rem(slot, CAP).astype(F32))
    rows = jnp.dot(
        jnp.where(placing, 1.0, 0.0).astype(BF), att_ref[...], preferred_element_type=F32
    ).astype(BF)
    half = rows.shape[1] // 2
    for e in range(E):
        for c in range(2):
            part = rows[e * CAP : (e + 1) * CAP, c * half : (c + 1) * half]
            for y in range(msg_ref.shape[1]):
                for x in range(msg_ref.shape[3]):
                    msg_ref[e, y, c, x] = part
    gate_matrix(ids_ref, gate_ref, mat_ref, msg_ref.shape[1] * msg_ref.shape[3])


def gate_matrix(ids_ref, gate_ref, mat_ref, copies):
    tok = ids_ref.shape[1]
    terms = E * copies * CAP
    same = lax.broadcasted_iota(jnp.int32, (tok, tok), 0) == lax.broadcasted_iota(jnp.int32, (tok, tok), 1)

    def column(ref, k):
        row = jnp.broadcast_to(ref[k : k + 1, :], (tok, tok))
        return jnp.sum(jnp.where(same, row, jnp.zeros_like(row)), axis=1, keepdims=True)

    lane = lax.broadcasted_iota(jnp.int32, (tok, terms), 1)
    expert = lax.div(lane, copies * CAP)
    first, second = column(ids_ref, 0) == expert, column(ids_ref, 1) == expert
    gate = jnp.where(first, column(gate_ref, 0), 0.0) + jnp.where(second, column(gate_ref, 1), 0.0)
    earlier = lax.broadcasted_iota(jnp.int32, (tok, tok), 1) < lax.broadcasted_iota(jnp.int32, (tok, tok), 0)
    rank = jnp.dot(
        jnp.where(earlier, 1.0, 0.0).astype(BF), jnp.where(first | second, 1.0, 0.0).astype(BF), preferred_element_type=F32
    )
    gate = jnp.where(rank == lax.rem(lane, CAP).astype(F32), gate, 0.0)
    high = gate.astype(BF)
    mat_ref[pl.ds(0, tok), :] = high
    mat_ref[pl.ds(tok, tok), :] = (gate - high.astype(F32)).astype(BF)


def home(recv, ids, gates, tp):
    tok, width = recv.shape[1], recv.shape[2] - 128
    return pl.pallas_call(
        home_kernel,
        out_shape=(
            jax.ShapeDtypeStruct((tok, width), BF),
            jax.ShapeDtypeStruct((E, 2, 2, tp, CAP, width // 2), BF),
            jax.ShapeDtypeStruct((2 * tok, E * 2 * tp * CAP), BF),
        ),
        in_specs=[VM] * 3,
        out_specs=(VM, VM, VM),
        compiler_params=pltpu.CompilerParams(vmem_limit_bytes=24 * MIB),
    )(recv, ids.T, gates.T)


def columns(x, side, half):
    return pl.ds(pl.multiple_of(x * 2 * half + side * half, half), half)


def this_core():
    return lax.rem(lax.axis_index("seq"), 2)


def start_rows(up_ref, w_buf, side, sems):
    half = w_buf.shape[1]
    copies = [pltpu.make_async_copy(up_ref.at[columns(x, side, half), :], w_buf.at[x], sems.at[x]) for x in range(w_buf.shape[0])]
    for copy in copies:
        copy.start()
    return copies


def start_columns(down_ref, d_buf, side, sems):
    half = d_buf.shape[2]
    copies = [pltpu.make_async_copy(down_ref.at[:, columns(x, side, half)], d_buf.at[x], sems.at[x]) for x in range(d_buf.shape[0])]
    for copy in copies:
        copy.start()
    return copies


def up_part(ref, side, gain_ref, s_buf, w_buf, copies, square):
    seqs, tp, cap, half = ref.shape
    for x in range(tp):
        a = ref[:, x].reshape(seqs * cap, half).astype(F32)
        s_buf[:, pl.ds(x * half, half)] = (a * gain_ref[:, columns(x, side, half)]).astype(BF)
        for c in range(half // 128):
            part = a[:, c * 128 : (c + 1) * 128]
            square = square + part * part
    for copy in copies:
        copy.wait()
    weights = w_buf[...].reshape(tp * half, w_buf.shape[2])
    return jnp.dot(s_buf[...], weights, preferred_element_type=F32), square


def up_first_kernel(own_ref, gain_ref, up_ref, total_ref, square_ref, s_buf, w_buf, sems):
    copies = start_rows(up_ref, w_buf, this_core(), sems)
    total, square = up_part(own_ref, this_core(), gain_ref, s_buf, w_buf, copies, jnp.zeros(square_ref.shape, F32))
    total_ref[...] = total
    square_ref[...] = square


def up_first(own, gain, w_up):
    rows, tp, half, hid = own.shape[0] * own.shape[2], own.shape[1], own.shape[3], w_up.shape[1]
    return pl.pallas_call(
        up_first_kernel,
        out_shape=(
            jax.ShapeDtypeStruct((rows, hid), F32),
            jax.ShapeDtypeStruct((rows, 128), F32),
        ),
        in_specs=[VM, VM, HBM],
        out_specs=(VM, VM),
        scratch_shapes=[
            pltpu.VMEM((rows, tp * half), BF),
            pltpu.VMEM((tp, half, hid), BF),
            pltpu.SemaphoreType.DMA((tp,)),
        ],
        compiler_params=pltpu.CompilerParams(vmem_limit_bytes=24 * MIB),
        cost_estimate=pl.CostEstimate(flops=2 * rows * tp * half * hid, bytes_accessed=5 * MIB, transcendentals=0),
    )(own, gain, w_up)


def up_second_kernel(
    other_ref, gain_ref, up_ref, down_ref, total_ref, square_ref, hidden_ref, send_ref, s_buf, w_buf, d_buf, sems, d_sems
):
    seqs, tp, cap, half = other_ref.shape
    other = 1 - this_core()
    copies = start_rows(up_ref, w_buf, other, sems)
    down_copies = start_columns(down_ref, d_buf, other, d_sems)
    total, square = up_part(other_ref, other, gain_ref, s_buf, w_buf, copies, square_ref[...])
    mean = jnp.sum(square, axis=1, keepdims=True) / (2 * tp * half)
    total = (total + total_ref[...]) * lax.rsqrt(mean + EPSILON)
    hidden = (total / (1.0 + jnp.exp(-total))).astype(BF)
    hidden_ref[...] = hidden
    for copy in down_copies:
        copy.wait()
    for x in range(tp):
        out = jnp.dot(hidden, d_buf[x], preferred_element_type=F32)
        send_ref[:, x] = out.astype(BF).reshape(seqs, cap, half)


def up_second(other, gain, w_up, w_down, total, square):
    rows, tp, half, hid = total.shape[0], other.shape[1], other.shape[3], w_up.shape[1]
    return pl.pallas_call(
        up_second_kernel,
        out_shape=(
            jax.ShapeDtypeStruct(total.shape, BF),
            jax.ShapeDtypeStruct(other.shape, BF),
        ),
        in_specs=[VM, VM, HBM, HBM, VM, VM],
        out_specs=(VM, VM),
        scratch_shapes=[
            pltpu.VMEM((rows, tp * half), BF),
            pltpu.VMEM((tp, half, hid), BF),
            pltpu.VMEM((tp, hid, half), BF),
            pltpu.SemaphoreType.DMA((tp,)),
            pltpu.SemaphoreType.DMA((tp,)),
        ],
        compiler_params=pltpu.CompilerParams(vmem_limit_bytes=30 * MIB),
    )(other, gain, w_up, w_down, total, square)


def down_kernel(hidden_ref, down_ref, out_ref, d_buf, sems):
    seqs, tp, cap, half = out_ref.shape
    copies = start_columns(down_ref, d_buf, this_core(), sems)
    hidden = hidden_ref[...]
    for copy in copies:
        copy.wait()
    for x in range(tp):
        out_ref[:, x] = jnp.dot(hidden, d_buf[x], preferred_element_type=F32).reshape(seqs, cap, half)


def down_project(hidden, w_down, shape):
    tp, half, hid = shape[1], shape[3], hidden.shape[1]
    return pl.pallas_call(
        down_kernel,
        out_shape=jax.ShapeDtypeStruct(shape, F32),
        in_specs=[VM, HBM],
        out_specs=VM,
        scratch_shapes=[pltpu.VMEM((tp, hid, half), BF), pltpu.SemaphoreType.DMA((tp,))],
        compiler_params=pltpu.CompilerParams(vmem_limit_bytes=24 * MIB),
        cost_estimate=pl.CostEstimate(flops=2 * hidden.shape[0] * tp * half * hid, bytes_accessed=5 * MIB, transcendentals=0),
    )(hidden, w_down)


def join_kernel(keep_ref, partner_ref, out_ref):
    for x in range(out_ref.shape[1]):
        out_ref[:, x] = (keep_ref[:, x] + partner_ref[:, x].astype(F32)).astype(BF)


def join(keep, partner):
    return pl.pallas_call(
        join_kernel,
        out_shape=jax.ShapeDtypeStruct(partner.shape, BF),
        in_specs=[VM] * 2,
        out_specs=VM,
        compiler_params=pltpu.CompilerParams(vmem_limit_bytes=16 * MIB),
    )(keep, partner)


def mix_kernel(recv_ref, mat_ref, out_ref):
    experts, pair, cores, tp, cap, half = recv_ref.shape
    tok = out_ref.shape[0]
    for c in range(cores):
        values = recv_ref[:, :, c].reshape(experts * pair * tp * cap, half)
        out = jnp.dot(mat_ref[...], values, preferred_element_type=F32)
        out_ref[:, pl.ds(c * half, half)] = (out[:tok] + out[tok:]).astype(BF)


def mix(recv, matrix):
    return pl.pallas_call(
        mix_kernel,
        out_shape=jax.ShapeDtypeStruct((matrix.shape[0] // 2, 2 * recv.shape[5]), BF),
        in_specs=[VM] * 2,
        out_specs=VM,
        compiler_params=pltpu.CompilerParams(vmem_limit_bytes=24 * MIB),
    )(recv, matrix)


def per_device(
    queries, cache_keys, cache_values, new_keys, new_values, reach, norm_gain, gate_weights, expert_ids, w_up, w_down
):
    seqs, tp = lax.axis_size("seq"), lax.axis_size("tp")
    seq = lax.axis_index("seq")
    core = lax.rem(seq, 2)
    tok, width = queries.shape
    chips = seqs // 2
    same_core = [list(range(c, seqs, 2)) for c in range(2)]
    swap = [(i, i ^ 1) for i in range(seqs)]

    def swapped(value):
        return lax.ppermute(value, "seq", swap)

    def moved(value, dz, dy):
        pairs = []
        for i in range(seqs):
            z, y, c = i // 2 // side, i // 2 % side, i % 2
            pairs.append((i, (((z - dz) % side) * side + (y - dy) % side) * 2 + c))
        return lax.ppermute(value, "seq", pairs)

    side = math.isqrt(chips)
    z, y = seq // 2 // side, seq // 2 % side
    near = jnp.concatenate([queries] + [moved(queries, 0, d) for d in range(1, side)], axis=0)
    far = [moved(near, d, 0) for d in range(1, side)]
    window = jnp.concatenate([new_keys, new_values], axis=0)
    own = [pltpu.with_memory_space_constraint(value, pltpu.HBM) for value in (cache_keys, cache_values)]
    rows_in = (*own, swapped(cache_keys), swapped(cache_values), window, swapped(window))
    limits = lax.dynamic_index_in_dim(reach.reshape(side, side, 2, tok), core, 2, keepdims=False)
    limits = jnp.concatenate([limits, limits], axis=0)
    limits = jnp.concatenate([limits, limits], axis=1)
    limits = lax.dynamic_slice(limits, (z, y, 0), (side, side, tok)).reshape(1, chips * tok)
    first = attention(limits[:, : side * tok], (near,), rows_in)
    outs = attention(limits[:, side * tok :], far, rows_in, first)
    arrived = lax.all_to_all(
        outs.reshape(chips, tok, outs.shape[1]), "seq", 0, 0, axis_index_groups=same_core, tiled=True
    )
    attended, message, matrix = home(arrived, expert_ids, gate_weights, tp)
    half = width // 2
    rows = lax.all_to_all(
        message.reshape(seqs * tp, CAP, half), ("seq", "tp"), 0, 0, tiled=True
    ).reshape(seqs, tp, CAP, half)
    gain = norm_gain.reshape(1, -1)
    up_rows = pltpu.with_memory_space_constraint(w_up[0], pltpu.HBM)
    down_rows = pltpu.with_memory_space_constraint(w_down[0], pltpu.HBM)
    total, square = up_first(rows, gain, up_rows)
    hidden, send = up_second(swapped(rows), gain, up_rows, down_rows, total, square)
    result = join(down_project(hidden, down_rows, send.shape), swapped(send))
    returned = lax.all_to_all(
        result.reshape(seqs * tp, CAP, half), ("seq", "tp"), 0, 0, tiled=True
    ).reshape(E, 2, 2, tp, CAP, half)
    return attended, mix(returned, matrix)


def solution(mesh):
    placed = (
        P("seq", "tp"),
        P("seq", "tp"),
        P("seq", "tp"),
        P("seq", "tp"),
        P("seq", "tp"),
        P(),
        P(),
        P("seq", None),
        P("seq", None),
        P("seq", None, "tp"),
        P("seq", "tp", None),
    )
    return jax.shard_map(
        per_device,
        mesh=mesh,
        in_specs=placed,
        out_specs=(P("seq", "tp"), P("seq", "tp")),
        check_vma=False,
    )
```

```python
import functools
import math

import jax
import jax.numpy as jnp
from jax import lax
from jax.experimental import pallas as pl
from jax.experimental.pallas import tpu as pltpu
from jax.sharding import PartitionSpec as P

HD = 128
E = 8
CAP = 16
EPSILON = 1e-05
NEG = -1e30
FLOOR = -1e20
BF = jnp.bfloat16
F32 = jnp.float32
SCALE = HD**-0.5 * math.log2(math.e)
MIB = 1024 * 1024
VM = pl.BlockSpec(memory_space=pltpu.VMEM)
HBM = pl.BlockSpec(memory_space=pltpu.HBM)

def attn_kernel(*refs, parts, earlier, per, CH):
    reach_ref = refs[0]
    q_refs, refs = refs[1 : 1 + parts], refs[1 + parts :]
    (k0_ref, v0_ref, k1_ref, v1_ref, n0_ref, n1_ref), refs = refs[:6], refs[6:]
    if earlier:
        prev_ref, refs = refs[0], refs[1:]
    o_ref, q_all, kk, vv, k_own, v_own, s_scr, m_scr, l_scr, lim_ref, tok_ref, sems = refs
    copies = [pltpu.make_async_copy(k0_ref, k_own, sems.at[0]), pltpu.make_async_copy(v0_ref, v_own, sems.at[1])]
    for copy in copies:
        copy.start(priority=1)
    tokens = q_refs[0].shape[0]
    W = n0_ref.shape[0] // 2
    blocks = tokens // W
    T = parts * tokens
    KEYS = k_own.shape[0]
    WIN = 2 * KEYS
    NCH = KEYS // CH
    R = per * tokens
    groups = 8 // per
    NT = parts * groups
    side = blocks
    seq = lax.axis_index("seq")
    core = lax.rem(seq, 2)
    partner = seq + 1 - 2 * core
    z, y = lax.div(seq, 2 * side), lax.rem(lax.div(seq, 2), side)

    def block(b):
        return lax.rem(z + b // side, side) * side + lax.rem(y + b % side, side)

    def fill(rows, keys, values):
        kk[rows, pl.ds(0, HD)] = keys
        kk[rows, pl.ds(HD, HD)] = keys
        vv[rows, pl.ds(0, HD)] = values
        vv[rows, pl.ds(HD, HD)] = jnp.ones_like(values)

    for p in range(parts):
        rows = pl.ds(p * tokens, tokens)
        q_all[rows, :] = q_refs[p][...]
        lim_ref[rows, :] = jnp.transpose(jnp.broadcast_to(reach_ref[:, p * tokens : (p + 1) * tokens], (128, tokens)))
    for b in range(T // W):
        tok_ref[pl.ds(b * W, W), :] = lax.broadcasted_iota(jnp.int32, (W, 128), 0) + (
            block(b + blocks * earlier) * 2 + core
        ) * W
    l_scr[...] = jnp.zeros_like(l_scr)
    if earlier:
        for b in range(blocks):
            o_ref[pl.ds(pl.multiple_of(block(b) * W, W), W), :] = prev_ref[pl.ds(b * W, W), :]
    fill(pl.ds(KEYS, KEYS), k1_ref[...], v1_ref[...])
    fill(pl.ds(WIN, W), n0_ref[pl.ds(0, W), :], n0_ref[pl.ds(W, W), :])
    fill(pl.ds(WIN + W, W), n1_ref[pl.ds(0, W), :], n1_ref[pl.ds(W, W), :])
    rest = pl.ds(WIN + 2 * W, 128 - 2 * W)
    fill(rest, jnp.zeros((128 - 2 * W, HD), BF), jnp.zeros((128 - 2 * W, HD), BF))
    for copy in copies:
        copy.wait()
    fill(pl.ds(0, KEYS), k_own[...], v_own[...])

    def target(i, b):
        if not earlier:
            return pl.multiple_of((lax.div(i, groups) * blocks + b) * W, W)
        place = lax.rem(z + lax.div(i, groups) + 1, side) * side + lax.rem(y + b, side)
        return pl.multiple_of(place * W, W)

    def tile(i):
        return pl.multiple_of(lax.div(i, groups) * tokens, tokens), lax.rem(i, groups) * per

    def repeated(x):
        return jnp.concatenate([x] * per, axis=0)

    def load_q(i):
        r, h = tile(i)
        out = []
        for k in range(per):
            qf = q_all[pl.ds(r, tokens), pl.ds(pl.multiple_of((h + k) * HD, HD), HD)].astype(F32) * SCALE
            hi = qf.astype(BF)
            out.append(jnp.concatenate([hi, (qf - hi.astype(F32)).astype(BF)], axis=1))
        return jnp.concatenate(out, axis=0)

    def dotk(qq, k):
        return lax.dot_general(qq, k, (((1,), (1,)), ((), ())), preferred_element_type=F32)

    def window_scores(i, qq):
        r, _ = tile(i)
        s = dotk(qq, kk[pl.ds(WIN, 128), :])
        lane = lax.broadcasted_iota(jnp.int32, (R, 128), 1)
        key = jnp.where(lane < W, lane + seq * W, lane - W + partner * W)
        return jnp.where((lane < 2 * W) & (key <= repeated(tok_ref[pl.ds(r, tokens), :])), s, NEG)

    def step(i, do_qk, do_pv):
        if do_qk:
            qq = load_q(i + 1)
            r1, _ = tile(i + 1)
            lim = repeated(lim_ref[pl.ds(r1, tokens), :])
            lane0 = lax.broadcasted_iota(jnp.int32, (R, 128), 1)
            sw = window_scores(i + 1, qq)
            mx = jnp.maximum(sw, FLOOR)
        if do_pv:
            m = m_scr[...]
            p = jnp.exp2(s_scr[:, pl.ds(WIN, 128)] - m)
            acc = jnp.dot(p.astype(BF), vv[pl.ds(WIN, 128), :], preferred_element_type=F32)
        if do_qk:
            s_scr[:, pl.ds(WIN, 128)] = sw
        for half in range(2):
            if do_qk:
                limh = lim - (seq, partner)[half] * KEYS
            for j in range(NCH):
                ks = half * KEYS + j * CH
                if do_pv:
                    p = jnp.concatenate(
                        [jnp.exp2(s_scr[:, pl.ds(ks + c * 128, 128)] - m).astype(BF) for c in range(CH // 128)], axis=1
                    )
                    acc = acc + jnp.dot(p, vv[pl.ds(ks, CH), :], preferred_element_type=F32)
                if do_qk:
                    s = dotk(qq, kk[pl.ds(ks, CH), :])
                    for c in range(CH // 128):
                        sc = jnp.where(lane0 + (j * CH + c * 128) < limh, s[:, c * 128 : (c + 1) * 128], NEG)
                        s_scr[:, pl.ds(ks + c * 128, 128)] = sc
                        mx = jnp.maximum(mx, sc)
        if do_pv:
            r, h = tile(i)
            l = acc[:, HD:]
            out = (acc[:, :HD] / jnp.maximum(l, 1.0)).astype(BF)
            L = jnp.where(l > 0, m + jnp.log2(jnp.maximum(l, 1e-30)), NEG)
            lane = lax.rem(lax.broadcasted_iota(jnp.int32, (tokens, 128), 1), 8)
            old = l_scr[pl.ds(r, tokens), :]
            for k in range(per):
                old = jnp.where(lane == h + k, L[k * tokens : (k + 1) * tokens], old)
                cols = pl.ds(pl.multiple_of((h + k) * HD, HD), HD)
                for b in range(blocks):
                    o_ref[pl.ds(target(i, b), W), cols] = out[k * tokens + b * W : k * tokens + (b + 1) * W]
            l_scr[pl.ds(r, tokens), :] = old
        if do_qk:
            m_scr[...] = jnp.broadcast_to(jnp.max(mx, axis=1, keepdims=True), (R, 128))

    step(jnp.int32(-1), True, False)

    def both(i, _):
        step(i, True, True)
        return 0

    lax.fori_loop(0, NT - 1, both, 0)
    step(jnp.int32(NT - 1), False, True)
    L = l_scr[...]
    hi = L.astype(BF).astype(F32)
    mid = (L - hi).astype(BF).astype(F32)
    lane = lax.broadcasted_iota(jnp.int32, L.shape, 1)
    packed = jnp.where(lane < 8, hi, jnp.where(lane < 16, mid, jnp.where(lane < 24, L - hi - mid, 0.0))).astype(BF)
    for b in range(T // W):
        place = block(b + blocks) if earlier else b
        o_ref[pl.ds(pl.multiple_of(place * W, W), W), pl.ds(8 * HD, 128)] = packed[b * W : (b + 1) * W]


def attention(reach, qs, tables, per, prev=None, CH=512):
    tokens = qs[0].shape[0]
    T = len(qs) * tokens
    keys = 2 * tables[0].shape[0] + 128
    rows = T + (0 if prev is None else tokens)
    more = () if prev is None else (prev,)
    return pl.pallas_call(
        functools.partial(attn_kernel, parts=len(qs), earlier=prev is not None, per=per, CH=CH),
        out_shape=jax.ShapeDtypeStruct((rows, 9 * HD), BF),
        in_specs=[VM] * (1 + len(qs)) + [HBM] * 2 + [VM] * (4 + len(more)),
        out_specs=VM,
        scratch_shapes=[
            pltpu.VMEM((T, 8 * HD), BF),
            pltpu.VMEM((keys, 2 * HD), BF),
            pltpu.VMEM((keys, 2 * HD), BF),
            pltpu.VMEM(tables[0].shape, BF),
            pltpu.VMEM(tables[0].shape, BF),
            pltpu.VMEM((per * tokens, keys), F32),
            pltpu.VMEM((per * tokens, 128), F32),
            pltpu.VMEM((T, 128), F32),
            pltpu.VMEM((T, 128), jnp.int32),
            pltpu.VMEM((T, 128), jnp.int32),
            pltpu.SemaphoreType.DMA((2,)),
        ],
        compiler_params=pltpu.CompilerParams(vmem_limit_bytes=(28 + 4 * per) * MIB),
        cost_estimate=pl.CostEstimate(flops=32 * T * keys * HD, bytes_accessed=8 * MIB, transcendentals=T * 8 * keys),
    )(reach, *qs, *tables, *more)


def home_kernel(recv_ref, ids_ref, gate_ref, att_ref, msg_ref, mat_ref):
    blocks, tok, _ = recv_ref.shape
    heads = att_ref.shape[1] // HD
    logs = []
    for s in range(blocks):
        tail = recv_ref[s, :, pl.ds(heads * HD, 128)].astype(F32)
        logs.append(tail + pltpu.roll(tail, 120, 1) + pltpu.roll(tail, 112, 1))
    top = functools.reduce(jnp.maximum, logs)
    shares = [jnp.exp2(x - top) for x in logs]
    inverse = 1.0 / functools.reduce(jnp.add, shares)
    shares = [x * inverse for x in shares]
    for h in range(heads):
        total = jnp.zeros((tok, HD), F32)
        for s in range(blocks):
            total = total + shares[s][:, h : h + 1] * recv_ref[s, :, pl.ds(h * HD, HD)].astype(F32)
        att_ref[:, pl.ds(h * HD, HD)] = total.astype(BF)
    slot = lax.broadcasted_iota(jnp.int32, (E * CAP, tok), 0)
    expert = lax.div(slot, CAP)
    member = (ids_ref[0:1, :] == expert) | (ids_ref[1:2, :] == expert)
    earlier = lax.broadcasted_iota(jnp.int32, (tok, tok), 0) < lax.broadcasted_iota(jnp.int32, (tok, tok), 1)
    rank = jnp.dot(
        jnp.where(member, 1.0, 0.0).astype(BF), jnp.where(earlier, 1.0, 0.0).astype(BF), preferred_element_type=F32
    )
    placing = member & (rank == lax.rem(slot, CAP).astype(F32))
    rows = jnp.dot(
        jnp.where(placing, 1.0, 0.0).astype(BF), att_ref[...], preferred_element_type=F32
    ).astype(BF)
    half = rows.shape[1] // 2
    for e in range(E):
        for c in range(2):
            part = rows[e * CAP : (e + 1) * CAP, c * half : (c + 1) * half]
            for y in range(msg_ref.shape[1]):
                for x in range(msg_ref.shape[3]):
                    msg_ref[e, y, c, x] = part
    gate_matrix(ids_ref, gate_ref, mat_ref, msg_ref.shape[1] * msg_ref.shape[3])


def gate_matrix(ids_ref, gate_ref, mat_ref, copies):
    tok = ids_ref.shape[1]
    terms = E * copies * CAP
    same = lax.broadcasted_iota(jnp.int32, (tok, tok), 0) == lax.broadcasted_iota(jnp.int32, (tok, tok), 1)

    def column(ref, k):
        row = jnp.broadcast_to(ref[k : k + 1, :], (tok, tok))
        return jnp.sum(jnp.where(same, row, jnp.zeros_like(row)), axis=1, keepdims=True)

    lane = lax.broadcasted_iota(jnp.int32, (tok, terms), 1)
    expert = lax.div(lane, copies * CAP)
    first, second = column(ids_ref, 0) == expert, column(ids_ref, 1) == expert
    gate = jnp.where(first, column(gate_ref, 0), 0.0) + jnp.where(second, column(gate_ref, 1), 0.0)
    earlier = lax.broadcasted_iota(jnp.int32, (tok, tok), 1) < lax.broadcasted_iota(jnp.int32, (tok, tok), 0)
    rank = jnp.dot(
        jnp.where(earlier, 1.0, 0.0).astype(BF), jnp.where(first | second, 1.0, 0.0).astype(BF), preferred_element_type=F32
    )
    gate = jnp.where(rank == lax.rem(lane, CAP).astype(F32), gate, 0.0)
    high = gate.astype(BF)
    mat_ref[pl.ds(0, tok), :] = high
    mat_ref[pl.ds(tok, tok), :] = (gate - high.astype(F32)).astype(BF)


def home(recv, ids, gates, tp):
    tok, width = recv.shape[1], recv.shape[2] - 128
    return pl.pallas_call(
        home_kernel,
        out_shape=(
            jax.ShapeDtypeStruct((tok, width), BF),
            jax.ShapeDtypeStruct((E, 2, 2, tp, CAP, width // 2), BF),
            jax.ShapeDtypeStruct((2 * tok, E * 2 * tp * CAP), BF),
        ),
        in_specs=[VM] * 3,
        out_specs=(VM, VM, VM),
        compiler_params=pltpu.CompilerParams(vmem_limit_bytes=24 * MIB),
    )(recv, ids.T, gates.T)


def columns(x, side, half):
    return pl.ds(pl.multiple_of(x * 2 * half + side * half, half), half)


def this_core():
    return lax.rem(lax.axis_index("seq"), 2)


def start_rows(up_ref, w_buf, side, sems):
    half = w_buf.shape[1]
    copies = [pltpu.make_async_copy(up_ref.at[columns(x, side, half), :], w_buf.at[x], sems.at[x]) for x in range(w_buf.shape[0])]
    for copy in copies:
        copy.start()
    return copies


def start_columns(down_ref, d_buf, side, sems):
    half = d_buf.shape[2]
    copies = [pltpu.make_async_copy(down_ref.at[:, columns(x, side, half)], d_buf.at[x], sems.at[x]) for x in range(d_buf.shape[0])]
    for copy in copies:
        copy.start()
    return copies


def up_part(ref, side, gain_ref, s_buf, w_buf, copies, square):
    seqs, tp, cap, half = ref.shape
    for x in range(tp):
        a = ref[:, x].reshape(seqs * cap, half).astype(F32)
        s_buf[:, pl.ds(x * half, half)] = (a * gain_ref[:, columns(x, side, half)]).astype(BF)
        for c in range(half // 128):
            part = a[:, c * 128 : (c + 1) * 128]
            square = square + part * part
    for copy in copies:
        copy.wait()
    weights = w_buf[...].reshape(tp * half, w_buf.shape[2])
    return jnp.dot(s_buf[...], weights, preferred_element_type=F32), square


def up_first_kernel(
    own_ref, gain_ref, up_ref, down_ref, total_ref, square_ref, next_up, next_down, s_buf, w_buf, sems, next_sems, down_sems
):
    copies = start_rows(up_ref, w_buf, this_core(), sems)
    later = start_rows(up_ref, next_up, 1 - this_core(), next_sems) + start_columns(down_ref, next_down, 1 - this_core(), down_sems)
    total, square = up_part(own_ref, this_core(), gain_ref, s_buf, w_buf, copies, jnp.zeros(square_ref.shape, F32))
    total_ref[...] = total
    square_ref[...] = square
    for copy in later:
        copy.wait()


def up_first(own, gain, w_up, w_down):
    rows, tp, half, hid = own.shape[0] * own.shape[2], own.shape[1], own.shape[3], w_up.shape[1]
    return pl.pallas_call(
        up_first_kernel,
        out_shape=(
            jax.ShapeDtypeStruct((rows, hid), F32),
            jax.ShapeDtypeStruct((rows, 128), F32),
            jax.ShapeDtypeStruct((tp, half, hid), BF),
            jax.ShapeDtypeStruct((tp, hid, half), BF),
        ),
        in_specs=[VM, VM, HBM, HBM],
        out_specs=(VM,) * 4,
        scratch_shapes=[
            pltpu.VMEM((rows, tp * half), BF),
            pltpu.VMEM((tp, half, hid), BF),
            pltpu.SemaphoreType.DMA((tp,)),
            pltpu.SemaphoreType.DMA((tp,)),
            pltpu.SemaphoreType.DMA((tp,)),
        ],
        compiler_params=pltpu.CompilerParams(vmem_limit_bytes=24 * MIB),
        cost_estimate=pl.CostEstimate(flops=2 * rows * tp * half * hid, bytes_accessed=5 * MIB, transcendentals=0),
    )(own, gain, w_up, w_down)


def up_second_kernel(other_ref, gain_ref, up_ref, down_ref, total_ref, square_ref, hidden_ref, send_ref):
    seqs, tp, cap, half = other_ref.shape
    total, square = total_ref[...], square_ref[...]
    for x in range(tp):
        a = other_ref[:, x].reshape(seqs * cap, half).astype(F32)
        scaled = (a * gain_ref[:, columns(x, 1 - this_core(), half)]).astype(BF)
        total = total + jnp.dot(scaled, up_ref[x], preferred_element_type=F32)
        for c in range(half // 128):
            part = a[:, c * 128 : (c + 1) * 128]
            square = square + part * part
    mean = jnp.sum(square, axis=1, keepdims=True) / (2 * tp * half)
    total = total * lax.rsqrt(mean + EPSILON)
    hidden = (total / (1.0 + jnp.exp(-total))).astype(BF)
    hidden_ref[...] = hidden
    for x in range(tp):
        out = jnp.dot(hidden, down_ref[x], preferred_element_type=F32)
        send_ref[:, x] = out.astype(BF).reshape(seqs, cap, half)


def up_second(other, gain, up_rows, down_columns, total, square):
    return pl.pallas_call(
        up_second_kernel,
        out_shape=(
            jax.ShapeDtypeStruct(total.shape, BF),
            jax.ShapeDtypeStruct(other.shape, BF),
        ),
        in_specs=[VM] * 6,
        out_specs=(VM, VM),
        compiler_params=pltpu.CompilerParams(vmem_limit_bytes=28 * MIB),
    )(other, gain, up_rows, down_columns, total, square)


def down_kernel(hidden_ref, down_ref, out_ref, d_buf, sems):
    seqs, tp, cap, half = out_ref.shape
    copies = start_columns(down_ref, d_buf, this_core(), sems)
    hidden = hidden_ref[...]
    for copy in copies:
        copy.wait()
    for x in range(tp):
        out_ref[:, x] = jnp.dot(hidden, d_buf[x], preferred_element_type=F32).reshape(seqs, cap, half)


def down_project(hidden, w_down, shape):
    tp, half, hid = shape[1], shape[3], hidden.shape[1]
    return pl.pallas_call(
        down_kernel,
        out_shape=jax.ShapeDtypeStruct(shape, F32),
        in_specs=[VM, HBM],
        out_specs=VM,
        scratch_shapes=[pltpu.VMEM((tp, hid, half), BF), pltpu.SemaphoreType.DMA((tp,))],
        compiler_params=pltpu.CompilerParams(vmem_limit_bytes=24 * MIB),
        cost_estimate=pl.CostEstimate(flops=2 * hidden.shape[0] * tp * half * hid, bytes_accessed=5 * MIB, transcendentals=0),
    )(hidden, w_down)


def join_kernel(keep_ref, partner_ref, out_ref):
    for x in range(out_ref.shape[1]):
        out_ref[:, x] = (keep_ref[:, x] + partner_ref[:, x].astype(F32)).astype(BF)


def join(keep, partner):
    return pl.pallas_call(
        join_kernel,
        out_shape=jax.ShapeDtypeStruct(partner.shape, BF),
        in_specs=[VM] * 2,
        out_specs=VM,
        compiler_params=pltpu.CompilerParams(vmem_limit_bytes=16 * MIB),
    )(keep, partner)


def mix_kernel(recv_ref, mat_ref, out_ref):
    experts, pair, cores, tp, cap, half = recv_ref.shape
    tok = out_ref.shape[0]
    for c in range(cores):
        values = recv_ref[:, :, c].reshape(experts * pair * tp * cap, half)
        out = jnp.dot(mat_ref[...], values, preferred_element_type=F32)
        out_ref[:, pl.ds(c * half, half)] = (out[:tok] + out[tok:]).astype(BF)


def mix(recv, matrix):
    return pl.pallas_call(
        mix_kernel,
        out_shape=jax.ShapeDtypeStruct((matrix.shape[0] // 2, 2 * recv.shape[5]), BF),
        in_specs=[VM] * 2,
        out_specs=VM,
        compiler_params=pltpu.CompilerParams(vmem_limit_bytes=24 * MIB),
    )(recv, matrix)


def per_device(
    queries, cache_keys, cache_values, new_keys, new_values, reach, norm_gain, gate_weights, expert_ids, w_up, w_down
):
    seqs, tp = lax.axis_size("seq"), lax.axis_size("tp")
    seq = lax.axis_index("seq")
    core = lax.rem(seq, 2)
    tok, width = queries.shape
    chips = seqs // 2
    same_core = [list(range(c, seqs, 2)) for c in range(2)]
    swap = [(i, i ^ 1) for i in range(seqs)]

    def swapped(value):
        return lax.ppermute(value, "seq", swap)

    def moved(value, dz, dy):
        pairs = []
        for i in range(seqs):
            z, y, c = i // 2 // side, i // 2 % side, i % 2
            pairs.append((i, (((z - dz) % side) * side + (y - dy) % side) * 2 + c))
        return lax.ppermute(value, "seq", pairs)

    side = math.isqrt(chips)
    z, y = seq // 2 // side, seq // 2 % side
    near = jnp.concatenate([queries] + [moved(queries, 0, d) for d in range(1, side)], axis=0)
    far = [moved(near, d, 0) for d in range(1, side)]
    window = jnp.concatenate([new_keys, new_values], axis=0)
    own = [pltpu.with_memory_space_constraint(value, pltpu.HBM) for value in (cache_keys, cache_values)]
    rows_in = (*own, swapped(cache_keys), swapped(cache_values), window, swapped(window))
    limits = lax.dynamic_index_in_dim(reach.reshape(side, side, 2, tok), core, 2, keepdims=False)
    limits = jnp.concatenate([limits, limits], axis=0)
    limits = jnp.concatenate([limits, limits], axis=1)
    limits = lax.dynamic_slice(limits, (z, y, 0), (side, side, tok)).reshape(1, chips * tok)
    first = attention(limits[:, : side * tok], (near,), rows_in, 2)
    outs = attention(limits[:, side * tok :], far, rows_in, 4, first)
    arrived = lax.all_to_all(
        outs.reshape(chips, tok, outs.shape[1]), "seq", 0, 0, axis_index_groups=same_core, tiled=True
    )
    attended, message, matrix = home(arrived, expert_ids, gate_weights, tp)
    half = width // 2
    rows = lax.all_to_all(
        message.reshape(seqs * tp, CAP, half), ("seq", "tp"), 0, 0, tiled=True
    ).reshape(seqs, tp, CAP, half)
    gain = norm_gain.reshape(1, -1)
    up_rows = pltpu.with_memory_space_constraint(w_up[0], pltpu.HBM)
    down_rows = pltpu.with_memory_space_constraint(w_down[0], pltpu.HBM)
    total, square, next_up, next_down = up_first(rows, gain, up_rows, down_rows)
    hidden, send = up_second(swapped(rows), gain, next_up, next_down, total, square)
    result = join(down_project(hidden, down_rows, send.shape), swapped(send))
    returned = lax.all_to_all(
        result.reshape(seqs * tp, CAP, half), ("seq", "tp"), 0, 0, tiled=True
    ).reshape(E, 2, 2, tp, CAP, half)
    return attended, mix(returned, matrix)


def solution(mesh):
    placed = (
        P("seq", "tp"),
        P("seq", "tp"),
        P("seq", "tp"),
        P("seq", "tp"),
        P("seq", "tp"),
        P(),
        P(),
        P("seq", None),
        P("seq", None),
        P("seq", None, "tp"),
        P("seq", "tp", None),
    )
    return jax.shard_map(
        per_device,
        mesh=mesh,
        in_specs=placed,
        out_specs=(P("seq", "tp"), P("seq", "tp")),
        check_vma=False,
    )
```

```python
import functools
import math

import jax
import jax.numpy as jnp
from jax import lax
from jax.experimental import pallas as pl
from jax.experimental.pallas import tpu as pltpu
from jax.sharding import PartitionSpec as P

HD = 128
E = 8
CAP = 16
EPSILON = 1e-05
NEG = -1e30
FLOOR = -1e20
BF = jnp.bfloat16
F32 = jnp.float32
SCALE = HD**-0.5 * math.log2(math.e)
MIB = 1024 * 1024
VM = pl.BlockSpec(memory_space=pltpu.VMEM)
HBM = pl.BlockSpec(memory_space=pltpu.HBM)

def attn_kernel(*refs, parts, earlier, per, CH):
    reach_ref = refs[0]
    q_refs, refs = refs[1 : 1 + parts], refs[1 + parts :]
    (k0_ref, v0_ref, k1_ref, v1_ref, n0_ref, n1_ref), refs = refs[:6], refs[6:]
    if earlier:
        prev_ref, refs = refs[0], refs[1:]
    o_ref, q_all, kk, vv, k_own, v_own, s_scr, m_scr, l_scr, lim_ref, tok_ref, sems = refs
    copies = [pltpu.make_async_copy(k0_ref, k_own, sems.at[0]), pltpu.make_async_copy(v0_ref, v_own, sems.at[1])]
    for copy in copies:
        copy.start(priority=1)
    tokens = q_refs[0].shape[0]
    W = n0_ref.shape[0] // 2
    blocks = tokens // W
    T = parts * tokens
    KEYS = k_own.shape[0]
    WIN = 2 * KEYS
    NCH = KEYS // CH
    R = per * tokens
    groups = 8 // per
    NT = parts * groups
    side = blocks
    seq = lax.axis_index("seq")
    core = lax.rem(seq, 2)
    partner = seq + 1 - 2 * core
    z, y = lax.div(seq, 2 * side), lax.rem(lax.div(seq, 2), side)

    def block(b):
        return lax.rem(z + b // side, side) * side + lax.rem(y + b % side, side)

    def fill(rows, keys, values):
        kk[rows, pl.ds(0, HD)] = keys
        kk[rows, pl.ds(HD, HD)] = keys
        vv[rows, pl.ds(0, HD)] = values
        vv[rows, pl.ds(HD, HD)] = jnp.ones_like(values)

    for p in range(parts):
        rows = pl.ds(p * tokens, tokens)
        q_all[rows, :] = q_refs[p][...]
        lim_ref[rows, :] = jnp.transpose(jnp.broadcast_to(reach_ref[:, p * tokens : (p + 1) * tokens], (128, tokens)))
    for b in range(T // W):
        tok_ref[pl.ds(b * W, W), :] = lax.broadcasted_iota(jnp.int32, (W, 128), 0) + (
            block(b + blocks * earlier) * 2 + core
        ) * W
    l_scr[...] = jnp.zeros_like(l_scr)
    if earlier:
        for b in range(blocks):
            o_ref[pl.ds(pl.multiple_of(block(b) * W, W), W), :] = prev_ref[pl.ds(b * W, W), :]
    fill(pl.ds(KEYS, KEYS), k1_ref[...], v1_ref[...])
    fill(pl.ds(WIN, W), n0_ref[pl.ds(0, W), :], n0_ref[pl.ds(W, W), :])
    fill(pl.ds(WIN + W, W), n1_ref[pl.ds(0, W), :], n1_ref[pl.ds(W, W), :])
    rest = pl.ds(WIN + 2 * W, 128 - 2 * W)
    fill(rest, jnp.zeros((128 - 2 * W, HD), BF), jnp.zeros((128 - 2 * W, HD), BF))
    for copy in copies:
        copy.wait()
    fill(pl.ds(0, KEYS), k_own[...], v_own[...])

    def target(i, b):
        if not earlier:
            return pl.multiple_of((lax.div(i, groups) * blocks + b) * W, W)
        place = lax.rem(z + lax.div(i, groups) + 1, side) * side + lax.rem(y + b, side)
        return pl.multiple_of(place * W, W)

    def tile(i):
        return pl.multiple_of(lax.div(i, groups) * tokens, tokens), lax.rem(i, groups) * per

    def repeated(x):
        return jnp.concatenate([x] * per, axis=0)

    def load_q(i):
        r, h = tile(i)
        out = []
        for k in range(per):
            qf = q_all[pl.ds(r, tokens), pl.ds(pl.multiple_of((h + k) * HD, HD), HD)].astype(F32) * SCALE
            hi = qf.astype(BF)
            out.append(jnp.concatenate([hi, (qf - hi.astype(F32)).astype(BF)], axis=1))
        return jnp.concatenate(out, axis=0)

    def dotk(qq, k):
        return lax.dot_general(qq, k, (((1,), (1,)), ((), ())), preferred_element_type=F32)

    def window_scores(i, qq):
        r, _ = tile(i)
        s = dotk(qq, kk[pl.ds(WIN, 128), :])
        lane = lax.broadcasted_iota(jnp.int32, (R, 128), 1)
        key = jnp.where(lane < W, lane + seq * W, lane - W + partner * W)
        return jnp.where((lane < 2 * W) & (key <= repeated(tok_ref[pl.ds(r, tokens), :])), s, NEG)

    def step(i, do_qk, do_pv):
        if do_qk:
            qq = load_q(i + 1)
            r1, _ = tile(i + 1)
            lim = repeated(lim_ref[pl.ds(r1, tokens), :])
            lane0 = lax.broadcasted_iota(jnp.int32, (R, 128), 1)
            sw = window_scores(i + 1, qq)
            mx = jnp.maximum(sw, FLOOR)
        if do_pv:
            m = m_scr[...]
            p = jnp.exp2(s_scr[:, pl.ds(WIN, 128)] - m)
            acc = jnp.dot(p.astype(BF), vv[pl.ds(WIN, 128), :], preferred_element_type=F32)
        if do_qk:
            s_scr[:, pl.ds(WIN, 128)] = sw
        for half in range(2):
            if do_qk:
                limh = lim - (seq, partner)[half] * KEYS
            for j in range(NCH):
                ks = half * KEYS + j * CH
                if do_pv:
                    p = jnp.concatenate(
                        [jnp.exp2(s_scr[:, pl.ds(ks + c * 128, 128)] - m).astype(BF) for c in range(CH // 128)], axis=1
                    )
                    acc = acc + jnp.dot(p, vv[pl.ds(ks, CH), :], preferred_element_type=F32)
                if do_qk:
                    s = dotk(qq, kk[pl.ds(ks, CH), :])
                    for c in range(CH // 128):
                        sc = jnp.where(lane0 + (j * CH + c * 128) < limh, s[:, c * 128 : (c + 1) * 128], NEG)
                        s_scr[:, pl.ds(ks + c * 128, 128)] = sc
                        mx = jnp.maximum(mx, sc)
        if do_pv:
            r, h = tile(i)
            l = acc[:, HD:]
            out = (acc[:, :HD] / jnp.maximum(l, 1.0)).astype(BF)
            L = jnp.where(l > 0, m + jnp.log2(jnp.maximum(l, 1e-30)), NEG)
            lane = lax.rem(lax.broadcasted_iota(jnp.int32, (tokens, 128), 1), 8)
            old = l_scr[pl.ds(r, tokens), :]
            for k in range(per):
                old = jnp.where(lane == h + k, L[k * tokens : (k + 1) * tokens], old)
                cols = pl.ds(pl.multiple_of((h + k) * HD, HD), HD)
                for b in range(blocks):
                    o_ref[pl.ds(target(i, b), W), cols] = out[k * tokens + b * W : k * tokens + (b + 1) * W]
            l_scr[pl.ds(r, tokens), :] = old
        if do_qk:
            m_scr[...] = jnp.broadcast_to(jnp.max(mx, axis=1, keepdims=True), (R, 128))

    step(jnp.int32(-1), True, False)

    def both(i, _):
        step(i, True, True)
        return 0

    lax.fori_loop(0, NT - 1, both, 0)
    step(jnp.int32(NT - 1), False, True)
    L = l_scr[...]
    hi = L.astype(BF).astype(F32)
    mid = (L - hi).astype(BF).astype(F32)
    lane = lax.broadcasted_iota(jnp.int32, L.shape, 1)
    packed = jnp.where(lane < 8, hi, jnp.where(lane < 16, mid, jnp.where(lane < 24, L - hi - mid, 0.0))).astype(BF)
    for b in range(T // W):
        place = block(b + blocks) if earlier else b
        o_ref[pl.ds(pl.multiple_of(place * W, W), W), pl.ds(8 * HD, 128)] = packed[b * W : (b + 1) * W]


def attention(reach, qs, tables, per, prev=None, CH=512):
    tokens = qs[0].shape[0]
    T = len(qs) * tokens
    keys = 2 * tables[0].shape[0] + 128
    rows = T + (0 if prev is None else tokens)
    more = () if prev is None else (prev,)
    return pl.pallas_call(
        functools.partial(attn_kernel, parts=len(qs), earlier=prev is not None, per=per, CH=CH),
        out_shape=jax.ShapeDtypeStruct((rows, 9 * HD), BF),
        in_specs=[VM] * (1 + len(qs)) + [HBM] * 2 + [VM] * (4 + len(more)),
        out_specs=VM,
        scratch_shapes=[
            pltpu.VMEM((T, 8 * HD), BF),
            pltpu.VMEM((keys, 2 * HD), BF),
            pltpu.VMEM((keys, 2 * HD), BF),
            pltpu.VMEM(tables[0].shape, BF),
            pltpu.VMEM(tables[0].shape, BF),
            pltpu.VMEM((per * tokens, keys), F32),
            pltpu.VMEM((per * tokens, 128), F32),
            pltpu.VMEM((T, 128), F32),
            pltpu.VMEM((T, 128), jnp.int32),
            pltpu.VMEM((T, 128), jnp.int32),
            pltpu.SemaphoreType.DMA((2,)),
        ],
        compiler_params=pltpu.CompilerParams(vmem_limit_bytes=(28 + 4 * per) * MIB),
        cost_estimate=pl.CostEstimate(flops=32 * T * keys * HD, bytes_accessed=8 * MIB, transcendentals=T * 8 * keys),
    )(reach, *qs, *tables, *more)


def home_kernel(recv_ref, ids_ref, att_ref, msg_ref):
    blocks, tok, _ = recv_ref.shape
    heads = att_ref.shape[1] // HD
    logs = []
    for s in range(blocks):
        tail = recv_ref[s, :, pl.ds(heads * HD, 128)].astype(F32)
        logs.append(tail + pltpu.roll(tail, 120, 1) + pltpu.roll(tail, 112, 1))
    top = functools.reduce(jnp.maximum, logs)
    shares = [jnp.exp2(x - top) for x in logs]
    inverse = 1.0 / functools.reduce(jnp.add, shares)
    shares = [x * inverse for x in shares]
    for h in range(heads):
        total = jnp.zeros((tok, HD), F32)
        for s in range(blocks):
            total = total + shares[s][:, h : h + 1] * recv_ref[s, :, pl.ds(h * HD, HD)].astype(F32)
        att_ref[:, pl.ds(h * HD, HD)] = total.astype(BF)
    slot = lax.broadcasted_iota(jnp.int32, (E * CAP, tok), 0)
    expert = lax.div(slot, CAP)
    member = (ids_ref[0:1, :] == expert) | (ids_ref[1:2, :] == expert)
    earlier = lax.broadcasted_iota(jnp.int32, (tok, tok), 0) < lax.broadcasted_iota(jnp.int32, (tok, tok), 1)
    rank = jnp.dot(
        jnp.where(member, 1.0, 0.0).astype(BF), jnp.where(earlier, 1.0, 0.0).astype(BF), preferred_element_type=F32
    )
    placing = member & (rank == lax.rem(slot, CAP).astype(F32))
    rows = jnp.dot(
        jnp.where(placing, 1.0, 0.0).astype(BF), att_ref[...], preferred_element_type=F32
    ).astype(BF)
    half = rows.shape[1] // 2
    for e in range(E):
        for c in range(2):
            part = rows[e * CAP : (e + 1) * CAP, c * half : (c + 1) * half]
            for y in range(msg_ref.shape[1]):
                for x in range(msg_ref.shape[3]):
                    msg_ref[e, y, c, x] = part


def gate_matrix(ids_ref, gate_ref, mat_ref, copies):
    tok = ids_ref.shape[1]
    terms = E * copies * CAP
    same = lax.broadcasted_iota(jnp.int32, (tok, tok), 0) == lax.broadcasted_iota(jnp.int32, (tok, tok), 1)

    def column(ref, k):
        row = jnp.broadcast_to(ref[k : k + 1, :], (tok, tok))
        return jnp.sum(jnp.where(same, row, jnp.zeros_like(row)), axis=1, keepdims=True)

    lane = lax.broadcasted_iota(jnp.int32, (tok, terms), 1)
    expert = lax.div(lane, copies * CAP)
    first, second = column(ids_ref, 0) == expert, column(ids_ref, 1) == expert
    gate = jnp.where(first, column(gate_ref, 0), 0.0) + jnp.where(second, column(gate_ref, 1), 0.0)
    earlier = lax.broadcasted_iota(jnp.int32, (tok, tok), 1) < lax.broadcasted_iota(jnp.int32, (tok, tok), 0)
    rank = jnp.dot(
        jnp.where(earlier, 1.0, 0.0).astype(BF), jnp.where(first | second, 1.0, 0.0).astype(BF), preferred_element_type=F32
    )
    gate = jnp.where(rank == lax.rem(lane, CAP).astype(F32), gate, 0.0)
    high = gate.astype(BF)
    mat_ref[pl.ds(0, tok), :] = high
    mat_ref[pl.ds(tok, tok), :] = (gate - high.astype(F32)).astype(BF)


def home(recv, ids, tp):
    tok, width = recv.shape[1], recv.shape[2] - 128
    return pl.pallas_call(
        home_kernel,
        out_shape=(
            jax.ShapeDtypeStruct((tok, width), BF),
            jax.ShapeDtypeStruct((E, 2, 2, tp, CAP, width // 2), BF),
        ),
        in_specs=[VM] * 2,
        out_specs=(VM, VM),
        compiler_params=pltpu.CompilerParams(vmem_limit_bytes=24 * MIB),
    )(recv, ids.T)


def columns(x, side, half):
    return pl.ds(pl.multiple_of(x * 2 * half + side * half, half), half)


def this_core():
    return lax.rem(lax.axis_index("seq"), 2)


def start_rows(up_ref, w_buf, side, sems):
    half = w_buf.shape[1]
    copies = [pltpu.make_async_copy(up_ref.at[columns(x, side, half), :], w_buf.at[x], sems.at[x]) for x in range(w_buf.shape[0])]
    for copy in copies:
        copy.start()
    return copies


def start_columns(down_ref, d_buf, side, sems):
    half = d_buf.shape[2]
    copies = [pltpu.make_async_copy(down_ref.at[:, columns(x, side, half)], d_buf.at[x], sems.at[x]) for x in range(d_buf.shape[0])]
    for copy in copies:
        copy.start()
    return copies


def up_part(ref, side, gain_ref, s_buf, w_buf, copies, square):
    seqs, tp, cap, half = ref.shape
    for x in range(tp):
        a = ref[:, x].reshape(seqs * cap, half).astype(F32)
        s_buf[:, pl.ds(x * half, half)] = (a * gain_ref[:, columns(x, side, half)]).astype(BF)
        for c in range(half // 128):
            part = a[:, c * 128 : (c + 1) * 128]
            square = square + part * part
    for copy in copies:
        copy.wait()
    weights = w_buf[...].reshape(tp * half, w_buf.shape[2])
    return jnp.dot(s_buf[...], weights, preferred_element_type=F32), square


def up_first_kernel(
    own_ref, gain_ref, up_ref, down_ref, total_ref, square_ref, next_up, next_down, s_buf, w_buf, sems, next_sems, down_sems
):
    copies = start_rows(up_ref, w_buf, this_core(), sems)
    later = start_rows(up_ref, next_up, 1 - this_core(), next_sems) + start_columns(down_ref, next_down, 1 - this_core(), down_sems)
    total, square = up_part(own_ref, this_core(), gain_ref, s_buf, w_buf, copies, jnp.zeros(square_ref.shape, F32))
    total_ref[...] = total
    square_ref[...] = square
    for copy in later:
        copy.wait()


def up_first(own, gain, w_up, w_down):
    rows, tp, half, hid = own.shape[0] * own.shape[2], own.shape[1], own.shape[3], w_up.shape[1]
    return pl.pallas_call(
        up_first_kernel,
        out_shape=(
            jax.ShapeDtypeStruct((rows, hid), F32),
            jax.ShapeDtypeStruct((rows, 128), F32),
            jax.ShapeDtypeStruct((tp, half, hid), BF),
            jax.ShapeDtypeStruct((tp, hid, half), BF),
        ),
        in_specs=[VM, VM, HBM, HBM],
        out_specs=(VM,) * 4,
        scratch_shapes=[
            pltpu.VMEM((rows, tp * half), BF),
            pltpu.VMEM((tp, half, hid), BF),
            pltpu.SemaphoreType.DMA((tp,)),
            pltpu.SemaphoreType.DMA((tp,)),
            pltpu.SemaphoreType.DMA((tp,)),
        ],
        compiler_params=pltpu.CompilerParams(vmem_limit_bytes=24 * MIB),
        cost_estimate=pl.CostEstimate(flops=2 * rows * tp * half * hid, bytes_accessed=5 * MIB, transcendentals=0),
    )(own, gain, w_up, w_down)


def up_second_kernel(other_ref, gain_ref, up_ref, down_ref, total_ref, square_ref, hidden_ref, send_ref):
    seqs, tp, cap, half = other_ref.shape
    total, square = total_ref[...], square_ref[...]
    for x in range(tp):
        a = other_ref[:, x].reshape(seqs * cap, half).astype(F32)
        scaled = (a * gain_ref[:, columns(x, 1 - this_core(), half)]).astype(BF)
        total = total + jnp.dot(scaled, up_ref[x], preferred_element_type=F32)
        for c in range(half // 128):
            part = a[:, c * 128 : (c + 1) * 128]
            square = square + part * part
    mean = jnp.sum(square, axis=1, keepdims=True) / (2 * tp * half)
    total = total * lax.rsqrt(mean + EPSILON)
    hidden = (total / (1.0 + jnp.exp(-total))).astype(BF)
    hidden_ref[...] = hidden
    for x in range(tp):
        out = jnp.dot(hidden, down_ref[x], preferred_element_type=F32)
        send_ref[:, x] = out.astype(BF).reshape(seqs, cap, half)


def up_second(other, gain, up_rows, down_columns, total, square):
    return pl.pallas_call(
        up_second_kernel,
        out_shape=(
            jax.ShapeDtypeStruct(total.shape, BF),
            jax.ShapeDtypeStruct(other.shape, BF),
        ),
        in_specs=[VM] * 6,
        out_specs=(VM, VM),
        compiler_params=pltpu.CompilerParams(vmem_limit_bytes=28 * MIB),
    )(other, gain, up_rows, down_columns, total, square)


def down_kernel(hidden_ref, down_ref, ids_ref, gate_ref, out_ref, mat_ref, d_buf, sems):
    seqs, tp, cap, half = out_ref.shape
    copies = start_columns(down_ref, d_buf, this_core(), sems)
    gate_matrix(ids_ref, gate_ref, mat_ref, 2 * tp)
    hidden = hidden_ref[...]
    for copy in copies:
        copy.wait()
    for x in range(tp):
        out_ref[:, x] = jnp.dot(hidden, d_buf[x], preferred_element_type=F32).reshape(seqs, cap, half)


def down_project(hidden, w_down, ids, gates, shape):
    tp, half, hid = shape[1], shape[3], hidden.shape[1]
    return pl.pallas_call(
        down_kernel,
        out_shape=(
            jax.ShapeDtypeStruct(shape, F32),
            jax.ShapeDtypeStruct((2 * ids.shape[0], E * 2 * tp * CAP), BF),
        ),
        in_specs=[VM, HBM, VM, VM],
        out_specs=(VM, VM),
        scratch_shapes=[pltpu.VMEM((tp, hid, half), BF), pltpu.SemaphoreType.DMA((tp,))],
        compiler_params=pltpu.CompilerParams(vmem_limit_bytes=24 * MIB),
        cost_estimate=pl.CostEstimate(flops=2 * hidden.shape[0] * tp * half * hid, bytes_accessed=5 * MIB, transcendentals=0),
    )(hidden, w_down, ids.T, gates.T)


def join_kernel(keep_ref, partner_ref, out_ref):
    for x in range(out_ref.shape[1]):
        out_ref[:, x] = (keep_ref[:, x] + partner_ref[:, x].astype(F32)).astype(BF)


def join(keep, partner):
    return pl.pallas_call(
        join_kernel,
        out_shape=jax.ShapeDtypeStruct(partner.shape, BF),
        in_specs=[VM] * 2,
        out_specs=VM,
        compiler_params=pltpu.CompilerParams(vmem_limit_bytes=16 * MIB),
    )(keep, partner)


def mix_kernel(recv_ref, mat_ref, out_ref):
    experts, pair, cores, tp, cap, half = recv_ref.shape
    tok = out_ref.shape[0]
    for c in range(cores):
        values = recv_ref[:, :, c].reshape(experts * pair * tp * cap, half)
        out = jnp.dot(mat_ref[...], values, preferred_element_type=F32)
        out_ref[:, pl.ds(c * half, half)] = (out[:tok] + out[tok:]).astype(BF)


def mix(recv, matrix):
    return pl.pallas_call(
        mix_kernel,
        out_shape=jax.ShapeDtypeStruct((matrix.shape[0] // 2, 2 * recv.shape[5]), BF),
        in_specs=[VM] * 2,
        out_specs=VM,
        compiler_params=pltpu.CompilerParams(vmem_limit_bytes=24 * MIB),
    )(recv, matrix)


def per_device(
    queries, cache_keys, cache_values, new_keys, new_values, reach, norm_gain, gate_weights, expert_ids, w_up, w_down
):
    seqs, tp = lax.axis_size("seq"), lax.axis_size("tp")
    seq = lax.axis_index("seq")
    core = lax.rem(seq, 2)
    tok, width = queries.shape
    chips = seqs // 2
    same_core = [list(range(c, seqs, 2)) for c in range(2)]
    swap = [(i, i ^ 1) for i in range(seqs)]

    def swapped(value):
        return lax.ppermute(value, "seq", swap)

    def moved(value, dz, dy):
        pairs = []
        for i in range(seqs):
            z, y, c = i // 2 // side, i // 2 % side, i % 2
            pairs.append((i, (((z - dz) % side) * side + (y - dy) % side) * 2 + c))
        return lax.ppermute(value, "seq", pairs)

    side = math.isqrt(chips)
    z, y = seq // 2 // side, seq // 2 % side
    near = jnp.concatenate([queries] + [moved(queries, 0, d) for d in range(1, side)], axis=0)
    far = [moved(near, d, 0) for d in range(1, side)]
    window = jnp.concatenate([new_keys, new_values], axis=0)
    own = [pltpu.with_memory_space_constraint(value, pltpu.HBM) for value in (cache_keys, cache_values)]
    rows_in = (*own, swapped(cache_keys), swapped(cache_values), window, swapped(window))
    limits = lax.dynamic_index_in_dim(reach.reshape(side, side, 2, tok), core, 2, keepdims=False)
    limits = jnp.concatenate([limits, limits], axis=0)
    limits = jnp.concatenate([limits, limits], axis=1)
    limits = lax.dynamic_slice(limits, (z, y, 0), (side, side, tok)).reshape(1, chips * tok)
    first = attention(limits[:, : side * tok], (near,), rows_in, 2)
    outs = attention(limits[:, side * tok :], far, rows_in, 4, first)
    arrived = lax.all_to_all(
        outs.reshape(chips, tok, outs.shape[1]), "seq", 0, 0, axis_index_groups=same_core, tiled=True
    )
    attended, message = home(arrived, expert_ids, tp)
    half = width // 2
    rows = lax.all_to_all(
        message.reshape(seqs * tp, CAP, half), ("seq", "tp"), 0, 0, tiled=True
    ).reshape(seqs, tp, CAP, half)
    gain = norm_gain.reshape(1, -1)
    up_rows = pltpu.with_memory_space_constraint(w_up[0], pltpu.HBM)
    down_rows = pltpu.with_memory_space_constraint(w_down[0], pltpu.HBM)
    total, square, next_up, next_down = up_first(rows, gain, up_rows, down_rows)
    hidden, send = up_second(swapped(rows), gain, next_up, next_down, total, square)
    kept, matrix = down_project(hidden, down_rows, expert_ids, gate_weights, send.shape)
    result = join(kept, swapped(send))
    returned = lax.all_to_all(
        result.reshape(seqs * tp, CAP, half), ("seq", "tp"), 0, 0, tiled=True
    ).reshape(E, 2, 2, tp, CAP, half)
    return attended, mix(returned, matrix)


def solution(mesh):
    placed = (
        P("seq", "tp"),
        P("seq", "tp"),
        P("seq", "tp"),
        P("seq", "tp"),
        P("seq", "tp"),
        P(),
        P(),
        P("seq", None),
        P("seq", None),
        P("seq", None, "tp"),
        P("seq", "tp", None),
    )
    return jax.shard_map(
        per_device,
        mesh=mesh,
        in_specs=placed,
        out_specs=(P("seq", "tp"), P("seq", "tp")),
        check_vma=False,
    )
```
